32 devices in a mesh: gx: 4 (over z), gy: 2 (over y), gz: 4 (over x, core).
Axes of the slice: x: 2, y: 2, z: 4, core: 2. Of those that a mesh axis runs over, the one named last changes fastest.
Arguments:
- fluid_velocity: float32 [3, 16, 16, 1024], P(None, 'gx', 'gy', 'gz'), may hold values from -6 to 6
- particle_velocity: float32 [2048, 3, 128], P(('gx', 'gy', 'gz')), may hold values from -4 to 4
- diameter: float32 [2048, 128], P(('gx', 'gy', 'gz')), may hold values from 0.4 to 0.7
- particle_cell: int32 [2048, 128], P(('gx', 'gy', 'gz')), may hold values from 0 to 8191
- block_owner: int32 [2048, 1], P(('gx', 'gy', 'gz')), may hold values from 0 to 7; in each aligned block of 64 rows (0 to 63, 64 to 127, ...) at most 32 rows name the same one
Outputs:
- particle_accel: float32 [2048, 3, 128], P(('gx', 'gy', 'gz'))
- voidage: float32 [16, 16, 1024], P('gx', 'gy', 'gz')
- fluid_next: float32 [3, 16, 16, 1024], P(None, 'gx', 'gy', 'gz')
The draws below stay inside these ranges and needn't reach their ends.
Inputs may be any that keep to these rules, and one draw needn't show every extreme that they name: `block_owner`: among the 64 blocks of one device at most 32 name one owner, and in every draw some device has exactly 32 blocks for some owner. An owner is a device of the same gz plane, numbered gx * 2 + gy. `particle_cell`: A cell of the owner's brick, numbered (x * 8 + y) * 256 + z in the brick's own coordinates.
All inputs are finite; a program needn't handle non-finite values.
Results may differ from the reference program's by a relative error of at most 0.00012.
Values sent between devices are 32-bit elements; how exact they have to be, the bound alone decides.
A program may use at most 128 MiB of HBM per device.

```python
import math
import jax
import jax.numpy as jnp
import numpy as np
from jax import lax

FX = 4
FY = 8
FZ = 256
BLK = 64
PB = 128
CAP = 32
CELLS_DEV = 8192
BLOCKS = 2048
NX = 16
NY = 16
NZ = 1024
N_GX = 4
N_GY = 2
N_GZ = 4


def with_ends(array, stream_key, smallest, largest):
    longest = array.shape.index(max(array.shape))
    spots = []
    for shift in (0, 1):
        where = [jax.random.randint(jax.random.fold_in(stream_key, axis), (), 0, length) for axis, length in enumerate(array.shape)]
        where[longest] = (where[longest] + shift) % array.shape[longest]
        spots.append(tuple(where))
    return array.at[spots[0]].set(smallest).at[spots[1]].set(largest)


def levels(stream_key, shape, shards, low, largest):
    gain, own = 1.0, jax.random.fold_in(stream_key, 6)
    for axis_at, shards_of in shards:
        draws = jnp.exp(jax.random.uniform(jax.random.fold_in(own, axis_at), (shards_of,), jnp.float32, low / len(shards), largest / len(shards)))
        gain = gain * jnp.repeat(draws, shape[axis_at] // shards_of).reshape([-1 if axis == axis_at else 1 for axis in range(len(shape))])
    return gain


def shared_out(stream_key, own, number, rows, amount, top, reach, skew):
    order = jax.random.permutation(stream_key, amount)
    heavy_load, common = load_shares(amount, rows * top, reach, skew, True), load_shares(amount, rows * top, reach, skew, False)
    places = jnp.arange(amount)

    def named(tallies, turn):
        used = int((tallies > 0).sum())
        fixed = max(1, used // 4)
        shifted = fixed + (places - fixed + turn * (used - fixed)) % max(1, amount - fixed)
        return jnp.zeros((amount,), jnp.int32).at[order[jnp.where(places < fixed, places, shifted)]].set(jnp.asarray(tallies, jnp.int32))

    tallies = jnp.where(number % 4 == 0, named(heavy_load, number // 4), named(common, number - number // 4 - 1))
    mixed = jax.random.permutation(jax.random.fold_in(own, 3), amount)
    giver, sink = mixed[0:amount // 2 * 2:2], mixed[1:amount // 2 * 2:2]
    slack = jnp.minimum(tallies[giver] - 1, reach - tallies[sink]) // 2
    slack = jnp.where((giver == order[0]) | (sink == order[0]) | (tallies[sink] == 0), 0, jnp.maximum(slack, 0))
    shifted = jax.random.randint(jax.random.fold_in(own, 4), (amount // 2,), 0, 1 << 20) % (slack + 1)
    tallies = tallies.at[giver].add(-shifted).at[sink].add(shifted)
    labels = jnp.searchsorted(jnp.cumsum(tallies), jnp.arange(rows * top), side="right").astype(jnp.int32)
    table = labels.reshape(top, rows).T
    table = table[jax.random.permutation(jax.random.fold_in(own, 1), rows)]
    turn = jax.random.randint(jax.random.fold_in(own, 2), (rows, 1), 0, top)
    return jnp.take_along_axis(table, (jnp.arange(top)[None, :] + turn) % top, axis=1)


def load_shares(amount, total, reach, lean, full):
    loads = [(1 << 20) // math.isqrt(rank ** lean) + 1 for rank in range(1, amount + 1)]
    largest = reach if full else min(reach, max(-(-total // amount), total * loads[0] // sum(loads)))
    least = 1 if total - largest >= amount - 1 else 0
    given, rest = [largest] + [least] * (amount - 1), total - largest - least * (amount - 1)
    while rest > 0:
        candidates = [i for i in range(1, amount) if given[i] < largest] or [i for i in range(1, amount) if given[i] < reach]
        mass, budget = sum([loads[i] for i in candidates]), rest
        for i in candidates:
            more = min(reach - given[i], max(1, budget * loads[i] // mass), rest)
            given[i] = given[i] + more
            rest = rest - more
    return np.array(given)


def normal_values(stream_key, dims, scale, reach, cuts=(), kind=jnp.bfloat16):
    result = scale * jax.random.normal(stream_key, dims, jnp.float32)
    if cuts:
        result = result * levels(stream_key, dims, cuts, -0.22, 0.18)
    return jnp.clip(result, -reach, reach).astype(kind)


def setup_inputs(seed: int = 0) -> dict:
    key_list = jax.random.split(jax.random.key(seed), 6)
    fluid_velocity = normal_values(key_list[0], (3, NX, NY, NZ), 1.0, 6.0, ((1, 4), (2, 2), (3, 4)), jnp.float32)
    particle_velocity = normal_values(key_list[1], (BLOCKS, 3, PB), 0.5, 4.0, ((0, 32),), jnp.float32)
    diameter = jnp.clip(0.4 + 0.29999998 * jax.random.uniform(key_list[2], (BLOCKS, PB), jnp.float32) ** levels(key_list[2], (BLOCKS, PB), ((0, 32),), -0.2, 0.2), 0.4, 0.7)
    particle_cell = with_ends(jax.random.randint(key_list[3], (BLOCKS, PB), 0, CELLS_DEV), jax.random.fold_in(key_list[3], 1), 0, CELLS_DEV - 1).astype(jnp.int32)
    block_owner_keys = jax.random.split(jax.random.fold_in(key_list[4], 1), BLOCKS // BLK)
    block_owner_turns = jax.random.permutation(jax.random.fold_in(key_list[4], 3), BLOCKS // BLK)
    block_owner = jax.vmap(lambda own, number: shared_out(jax.random.fold_in(key_list[4], 2), own, number, BLK, N_GX * N_GY, 1, CAP, 2))(block_owner_keys, block_owner_turns).reshape((BLOCKS, 1))
    return dict(fluid_velocity=fluid_velocity, particle_velocity=particle_velocity, diameter=diameter, particle_cell=particle_cell, block_owner=block_owner)


VISCOSITY = 0.1
FLUID_DENSITY = 0.05
SOLID_DENSITY = 2.5
TIME_STEP = 0.05
VOID_FLOOR = 0.35
SPREAD = 0.1

def pad_grid(field):
    widths = [(0, 0)] * (field.ndim - 3) + [(1, 1)] * 3
    return jnp.pad(field, widths)

def neighbours(padded):
    total = padded[..., 2:, 1:-1, 1:-1] + padded[..., :-2, 1:-1, 1:-1]
    total = total + padded[..., 1:-1, 2:, 1:-1] + padded[..., 1:-1, :-2, 1:-1]
    return total + padded[..., 1:-1, 1:-1, 2:] + padded[..., 1:-1, 1:-1, :-2]

def drag_force(slip, diam_part, void_at):
    slip_speed = jnp.sqrt(lax.optimization_barrier(jnp.sum(slip * slip, axis=1)))
    reynolds = jnp.maximum(void_at * diam_part * slip_speed / VISCOSITY, 1.0)
    drag_coeff = (0.63 + 4.8 / jnp.sqrt(reynolds)) ** 2
    chi_exp = 3.7 - 0.65 * jnp.exp(-0.5 * (1.5 - jnp.log10(reynolds)) ** 2)
    magnitude = 0.5 * drag_coeff * FLUID_DENSITY * (math.pi / 4) * diam_part * diam_part
    magnitude = magnitude * jnp.exp((2.0 - chi_exp) * jnp.log(void_at)) * slip_speed
    return magnitude[:, None, :] * slip

def reference(fluid_velocity, particle_velocity, diameter, particle_cell, block_owner):
    blocks = diameter.shape[0]
    device_of = jnp.arange(blocks, dtype=jnp.int32) // BLK
    plane_gz = device_of % N_GZ
    owner_of = block_owner[:, 0]
    owner_gx = owner_of // N_GY
    owner_gy = owner_of % N_GY
    local_x = particle_cell // (FY * FZ)
    local_y = particle_cell // FZ % FY
    local_z = particle_cell % FZ
    glob_x = owner_gx[:, None] * FX + local_x
    glob_y = owner_gy[:, None] * FY + local_y
    glob_z = plane_gz[:, None] * FZ + local_z
    flat_cell = ((glob_x * NY + glob_y) * NZ + glob_z).astype(jnp.int32)
    total_cells = NX * NY * NZ
    volume = math.pi / 6 * diameter * diameter * diameter
    solid = jax.ops.segment_sum(volume.ravel(), flat_cell.ravel(), num_segments=total_cells).reshape(NX, NY, NZ)
    smooth = (solid + SPREAD * neighbours(pad_grid(solid))) / (1.0 + 6 * SPREAD)
    voidage = jnp.maximum(1.0 - smooth, VOID_FLOOR)
    flat_u = fluid_velocity.reshape(3, total_cells)
    u_at = jnp.moveaxis(jnp.take(flat_u, flat_cell, axis=1), 0, 1)
    void_at = voidage.reshape(total_cells)[flat_cell]
    force = drag_force(u_at - particle_velocity, diameter, void_at)
    particle_accel = force / (SOLID_DENSITY * volume)[:, None, :]
    source = -jnp.stack([jax.ops.segment_sum(force[:, component].ravel(), flat_cell.ravel(), num_segments=total_cells) for component in range(3)])
    source = source.reshape(3, NX, NY, NZ)
    laplace = neighbours(pad_grid(fluid_velocity)) - 6.0 * fluid_velocity
    fluid_next = fluid_velocity + TIME_STEP * (laplace + source / (FLUID_DENSITY * voidage)[None])
    return (particle_accel, voidage, fluid_next)
```

```python
import functools
import math

import jax
import jax.numpy as jnp
from jax import lax
from jax.experimental import pallas as pl
from jax.experimental.pallas import tpu as pltpu
from jax.sharding import PartitionSpec as P

VISCOSITY = 0.1
FLUID_DENSITY = 0.05
SOLID_DENSITY = 2.5
TIME_STEP = 0.05
VOID_FLOOR = 0.35
SPREAD = 0.1
GROUP = 8
PLANE = ("gx", "gy")
VMEM = pltpu.MemorySpace.VMEM
SMEM = pltpu.MemorySpace.SMEM


def halves(value):
    high = value.astype(jnp.bfloat16)
    low = (value - high.astype(jnp.float32)).astype(jnp.bfloat16)
    return high, low


def lane_onehot(cell_row, lane_count, per_block):
    lanes = lax.broadcasted_iota(jnp.int32, (lane_count, per_block), 0)
    hit = lanes == (cell_row & (lane_count - 1))
    return jnp.where(hit, 1.0, 0.0).astype(jnp.bfloat16)


def row_hits(cell_row, row_count, lane_count, per_block):
    rows = lax.broadcasted_iota(jnp.int32, (row_count, per_block), 0)
    return rows == lax.shift_right_logical(cell_row, lane_count.bit_length() - 1)


def spread_rows(hits, values):
    pieces = [halves(value) for value in values]
    stacked = [jnp.where(hits, part[0].astype(jnp.float32), 0.0) for part in pieces]
    stacked += [jnp.where(hits, part[1].astype(jnp.float32), 0.0) for part in pieces]
    return jnp.concatenate(stacked, axis=0).astype(jnp.bfloat16)


def onto_cells(rows, lane_hot):
    both = lax.dot_general(
        rows, lane_hot, (((1,), (1,)), ((), ())), preferred_element_type=jnp.float32
    )
    half = both.shape[0] // 2
    return both[:half] + both[half:]


def volume_kernel(owner_ref, cell_ref, diam_ref, out_ref):
    blocks, per_block = cell_ref.shape
    row_count, lane_count = out_ref.shape[1:]
    out_ref[...] = jnp.zeros_like(out_ref)

    @pl.loop(0, blocks // GROUP)
    def _(group):
        start = pl.multiple_of(group * GROUP, GROUP)
        cells = cell_ref[pl.ds(start, GROUP), :]
        diam = diam_ref[pl.ds(start, GROUP), :]
        volume = math.pi / 6 * diam * diam * diam
        adds = []
        for i in range(GROUP):
            row = cells[i : i + 1]
            hits = row_hits(row, row_count, lane_count, per_block)
            rows = spread_rows(hits, [volume[i : i + 1]])
            adds.append(onto_cells(rows, lane_onehot(row, lane_count, per_block)))
        for i in range(GROUP):
            owner = owner_ref[start + i]
            out_ref[owner] = out_ref[owner] + adds[i]


def force_kernel(
    owner_ref, cell_ref, diam_ref, part_ref, vel_ref, void_ref, accel_ref, out_ref, table
):
    blocks, per_block = cell_ref.shape
    owners, row_count, lane_count = void_ref.shape
    out_ref[...] = jnp.zeros_like(out_ref)

    @pl.loop(0, owners)
    def _(owner):
        both = jnp.concatenate([vel_ref[owner], void_ref[owner]], axis=0)
        high, low = halves(both)
        table[owner] = jnp.concatenate([high, low], axis=0)

    @pl.loop(0, blocks // GROUP)
    def _(group):
        start = pl.multiple_of(group * GROUP, GROUP)
        cells = cell_ref[pl.ds(start, GROUP), :]
        diam = diam_ref[pl.ds(start, GROUP), :]
        hots, hit_list, looked = [], [], [[], [], [], []]
        for i in range(GROUP):
            row = cells[i : i + 1]
            hot = lane_onehot(row, lane_count, per_block)
            hits = row_hits(row, row_count, lane_count, per_block)
            hots.append(hot)
            hit_list.append(hits)
            both = jnp.dot(
                table[owner_ref[start + i]], hot, preferred_element_type=jnp.float32
            )
            half = both.shape[0] // 2
            both = both[:half] + both[half:]
            for comp in range(4):
                piece = both[comp * row_count : (comp + 1) * row_count]
                looked[comp].append(
                    jnp.sum(jnp.where(hits, piece, 0.0), axis=0, keepdims=True)
                )
        at = [jnp.concatenate(rows, axis=0) for rows in looked]
        slip = [at[comp] - part_ref[pl.ds(start, GROUP), comp, :] for comp in range(3)]
        void_at = at[3]
        speed = jnp.sqrt(slip[0] * slip[0] + slip[1] * slip[1] + slip[2] * slip[2])
        reynolds = jnp.maximum(void_at * diam * speed / VISCOSITY, 1.0)
        drag_coeff = 0.63 + 4.8 / jnp.sqrt(reynolds)
        drag_coeff = drag_coeff * drag_coeff
        gap = 1.5 - jnp.log(reynolds) * (1.0 / math.log(10.0))
        chi_exp = 3.7 - 0.65 * jnp.exp(-0.5 * gap * gap)
        magnitude = 0.5 * drag_coeff * FLUID_DENSITY * (math.pi / 4) * diam * diam
        magnitude = magnitude * jnp.exp((2.0 - chi_exp) * jnp.log(void_at)) * speed
        force = [magnitude * slip[comp] for comp in range(3)]
        mass = SOLID_DENSITY * (math.pi / 6 * diam * diam * diam)
        for comp in range(3):
            accel_ref[pl.ds(start, GROUP), comp, :] = force[comp] / mass
        adds = []
        for i in range(GROUP):
            rows = spread_rows(hit_list[i], [force[comp][i : i + 1] for comp in range(3)])
            adds.append(onto_cells(rows, hots[i]))
        for i in range(GROUP):
            owner = owner_ref[start + i]
            out_ref[owner] = out_ref[owner] + adds[i]


def neighbours(padded):
    total = padded[..., 2:, 1:-1, 1:-1] + padded[..., :-2, 1:-1, 1:-1]
    total = total + padded[..., 1:-1, 2:, 1:-1] + padded[..., 1:-1, :-2, 1:-1]
    return total + padded[..., 1:-1, 1:-1, 2:] + padded[..., 1:-1, 1:-1, :-2]


def with_edges(cells):
    count = lax.axis_size("gz")
    up = [(i, i + 1) for i in range(count - 1)]
    down = [(i + 1, i) for i in range(count - 1)]
    return jnp.concatenate(
        [
            lax.ppermute(cells[..., -1:], "gz", up),
            cells,
            lax.ppermute(cells[..., :1], "gz", down),
        ],
        axis=-1,
    )


def per_device(fluid_velocity, particle_velocity, diameter, particle_cell, block_owner):
    size_x, size_y = lax.axis_size("gx"), lax.axis_size("gy")
    owners = size_x * size_y
    bx, by, lane_count = fluid_velocity.shape[1:]
    row_count = bx * by
    at_x, at_y = lax.axis_index("gx") * bx, lax.axis_index("gy") * by
    owner_list = block_owner[:, 0]
    limit = 56 * 1024 * 1024

    partial = pl.pallas_call(
        volume_kernel,
        out_shape=jax.ShapeDtypeStruct((owners, row_count, lane_count), jnp.float32),
        in_specs=[pl.BlockSpec(memory_space=SMEM)] + [pl.BlockSpec(memory_space=VMEM)] * 2,
        out_specs=pl.BlockSpec(memory_space=VMEM),
        compiler_params=pltpu.CompilerParams(vmem_limit_bytes=limit),
        name="volume_deposit",
    )(owner_list, particle_cell, diameter)

    vel_edges = with_edges(fluid_velocity)
    vel_all = lax.all_gather(fluid_velocity.reshape(3 * row_count, lane_count), PLANE)

    parts = lax.all_to_all(partial, PLANE, split_axis=0, concat_axis=0, tiled=True)
    solid = jnp.sum(parts, axis=0).reshape(bx, by, lane_count)
    solid_all = lax.all_gather(with_edges(solid), PLANE)
    plane = solid_all.reshape(size_x, size_y, bx, by, lane_count + 2)
    plane = plane.transpose(0, 2, 1, 3, 4).reshape(size_x * bx, size_y * by, lane_count + 2)
    plane = jnp.pad(plane, ((1, 1), (1, 1), (0, 0)))
    smooth = (plane[1:-1, 1:-1, 1:-1] + SPREAD * neighbours(plane)) / (1.0 + 6 * SPREAD)
    void_plane = jnp.maximum(1.0 - smooth, VOID_FLOOR)
    voidage = lax.dynamic_slice(void_plane, (at_x, at_y, 0), (bx, by, lane_count))
    void_all = void_plane.reshape(size_x, bx, size_y, by, lane_count)
    void_all = void_all.transpose(0, 2, 1, 3, 4).reshape(owners, row_count, lane_count)

    accel, force_part = pl.pallas_call(
        force_kernel,
        out_shape=(
            jax.ShapeDtypeStruct(particle_velocity.shape, jnp.float32),
            jax.ShapeDtypeStruct((owners, 3 * row_count, lane_count), jnp.float32),
        ),
        in_specs=[pl.BlockSpec(memory_space=SMEM)] + [pl.BlockSpec(memory_space=VMEM)] * 5,
        out_specs=(pl.BlockSpec(memory_space=VMEM),) * 2,
        scratch_shapes=[pltpu.VMEM((owners, 8 * row_count, lane_count), jnp.bfloat16)],
        compiler_params=pltpu.CompilerParams(vmem_limit_bytes=limit),
        name="force_deposit",
    )(owner_list, particle_cell, diameter, particle_velocity, vel_all, void_all)

    forces = lax.all_to_all(force_part, PLANE, split_axis=0, concat_axis=0, tiled=True)
    source = -jnp.sum(forces, axis=0).reshape(3, bx, by, lane_count)

    vel_plane = vel_all.reshape(size_x, size_y, 3, bx, by, lane_count)
    vel_plane = vel_plane.transpose(2, 0, 3, 1, 4, 5)
    vel_plane = vel_plane.reshape(3, size_x * bx, size_y * by, lane_count)
    vel_plane = jnp.pad(vel_plane, ((0, 0), (1, 1), (1, 1), (0, 0)))
    near = lax.dynamic_slice(
        vel_plane, (0, at_x, at_y, 0), (3, bx + 2, by + 2, lane_count)
    )
    total = near[:, 2:, 1:-1] + near[:, :-2, 1:-1] + near[:, 1:-1, 2:] + near[:, 1:-1, :-2]
    total = total + vel_edges[..., 2:] + vel_edges[..., :-2]
    laplace = total - 6.0 * fluid_velocity
    fluid_next = fluid_velocity + TIME_STEP * (laplace + source / (FLUID_DENSITY * voidage)[None])
    return (accel, voidage, fluid_next)


def solution(mesh):
    placed = (
        P(None, "gx", "gy", "gz"),
        P(("gx", "gy", "gz"), None, None),
        P(("gx", "gy", "gz"), None),
        P(("gx", "gy", "gz"), None),
        P(("gx", "gy", "gz"), None),
    )
    return jax.shard_map(
        per_device,
        mesh=mesh,
        in_specs=placed,
        out_specs=(
            P(("gx", "gy", "gz"), None, None),
            P("gx", "gy", "gz"),
            P(None, "gx", "gy", "gz"),
        ),
        check_vma=False,
    )
```

```python
import functools
import math

import jax
import jax.numpy as jnp
from jax import lax
from jax.experimental import pallas as pl
from jax.experimental.pallas import tpu as pltpu
from jax.sharding import PartitionSpec as P

VISCOSITY = 0.1
FLUID_DENSITY = 0.05
SOLID_DENSITY = 2.5
TIME_STEP = 0.05
VOID_FLOOR = 0.35
SPREAD = 0.1
GROUP = 8
PLANE = ("gx", "gy")
VMEM = pltpu.MemorySpace.VMEM
SMEM = pltpu.MemorySpace.SMEM


def halves(value):
    high = value.astype(jnp.bfloat16)
    low = (value - high.astype(jnp.float32)).astype(jnp.bfloat16)
    return high, low


def lane_onehot(cell_row, lane_count, per_block):
    lanes = lax.broadcasted_iota(jnp.int32, (lane_count, per_block), 0)
    hit = lanes == (cell_row & (lane_count - 1))
    return jnp.where(hit, 1.0, 0.0).astype(jnp.bfloat16)


def row_hits(cell_row, row_count, lane_count, per_block):
    rows = lax.broadcasted_iota(jnp.int32, (row_count, per_block), 0)
    return rows == lax.shift_right_logical(cell_row, lane_count.bit_length() - 1)


def spread_rows(hits, values):
    pieces = [halves(value) for value in values]
    stacked = [jnp.where(hits, part[0].astype(jnp.float32), 0.0) for part in pieces]
    stacked += [jnp.where(hits, part[1].astype(jnp.float32), 0.0) for part in pieces]
    return jnp.concatenate(stacked, axis=0).astype(jnp.bfloat16)


def onto_cells(rows, lane_hot):
    both = lax.dot_general(
        rows, lane_hot, (((1,), (1,)), ((), ())), preferred_element_type=jnp.float32
    )
    half = both.shape[0] // 2
    return both[:half] + both[half:]


def volume_kernel(owner_ref, cell_ref, diam_ref, out_ref):
    blocks, per_block = cell_ref.shape
    row_count, lane_count = out_ref.shape[1:]
    out_ref[...] = jnp.zeros_like(out_ref)

    @pl.loop(0, blocks // GROUP)
    def _(group):
        start = pl.multiple_of(group * GROUP, GROUP)
        cells = cell_ref[pl.ds(start, GROUP), :]
        diam = diam_ref[pl.ds(start, GROUP), :]
        volume = math.pi / 6 * diam * diam * diam
        adds = []
        for i in range(GROUP):
            row = cells[i : i + 1]
            hits = row_hits(row, row_count, lane_count, per_block)
            rows = spread_rows(hits, [volume[i : i + 1]])
            adds.append(onto_cells(rows, lane_onehot(row, lane_count, per_block)))
        for i in range(GROUP):
            owner = owner_ref[start + i]
            out_ref[owner] = out_ref[owner] + adds[i]


def force_kernel(
    owner_ref, cell_ref, diam_ref, part_ref, vel_ref, void_ref, accel_ref, out_ref, table
):
    blocks, per_block = cell_ref.shape
    owners, row_count, lane_count = void_ref.shape
    out_ref[...] = jnp.zeros_like(out_ref)

    @pl.loop(0, owners)
    def _(owner):
        both = jnp.concatenate([vel_ref[owner], void_ref[owner]], axis=0)
        high, low = halves(both)
        table[owner] = jnp.concatenate([high, low], axis=0)

    @pl.loop(0, blocks // GROUP)
    def _(group):
        start = pl.multiple_of(group * GROUP, GROUP)
        cells = cell_ref[pl.ds(start, GROUP), :]
        diam = diam_ref[pl.ds(start, GROUP), :]
        hots, hit_list, looked = [], [], [[], [], [], []]
        for i in range(GROUP):
            row = cells[i : i + 1]
            hot = lane_onehot(row, lane_count, per_block)
            hits = row_hits(row, row_count, lane_count, per_block)
            hots.append(hot)
            hit_list.append(hits)
            both = jnp.dot(
                table[owner_ref[start + i]], hot, preferred_element_type=jnp.float32
            )
            half = both.shape[0] // 2
            both = both[:half] + both[half:]
            for comp in range(4):
                piece = both[comp * row_count : (comp + 1) * row_count]
                looked[comp].append(
                    jnp.sum(jnp.where(hits, piece, 0.0), axis=0, keepdims=True)
                )
        at = [jnp.concatenate(rows, axis=0) for rows in looked]
        slip = [at[comp] - part_ref[pl.ds(start, GROUP), comp, :] for comp in range(3)]
        void_at = at[3]
        speed = jnp.sqrt(slip[0] * slip[0] + slip[1] * slip[1] + slip[2] * slip[2])
        reynolds = jnp.maximum(void_at * diam * speed / VISCOSITY, 1.0)
        drag_coeff = 0.63 + 4.8 / jnp.sqrt(reynolds)
        drag_coeff = drag_coeff * drag_coeff
        gap = 1.5 - jnp.log(reynolds) * (1.0 / math.log(10.0))
        chi_exp = 3.7 - 0.65 * jnp.exp(-0.5 * gap * gap)
        magnitude = 0.5 * drag_coeff * FLUID_DENSITY * (math.pi / 4) * diam * diam
        magnitude = magnitude * jnp.exp((2.0 - chi_exp) * jnp.log(void_at)) * speed
        force = [magnitude * slip[comp] for comp in range(3)]
        mass = SOLID_DENSITY * (math.pi / 6 * diam * diam * diam)
        for comp in range(3):
            accel_ref[pl.ds(start, GROUP), comp, :] = force[comp] / mass
        adds = []
        for i in range(GROUP):
            rows = spread_rows(hit_list[i], [force[comp][i : i + 1] for comp in range(3)])
            adds.append(onto_cells(rows, hots[i]))
        for i in range(GROUP):
            owner = owner_ref[start + i]
            out_ref[owner] = out_ref[owner] + adds[i]


def each(first, last, body):
    def step(i, carry):
        body(i)
        return carry

    lax.fori_loop(first, last, step, 0)


def remote(src, dst, send_sem, recv_sem, device):
    return pltpu.make_async_remote_copy(
        src_ref=src,
        dst_ref=dst,
        send_sem=send_sem,
        recv_sem=recv_sem,
        device_id=device,
        device_id_type=pl.DeviceIdType.MESH,
    )


def signal(semaphore, device):
    pl.semaphore_signal(
        semaphore, inc=1, device_id=device, device_id_type=pl.DeviceIdType.MESH
    )


def shifted(cells, axis, step, outside):
    size = cells.shape[axis]
    if step > 0:
        kept = lax.slice_in_dim(cells, 0, size - 1, axis=axis)
        return jnp.concatenate([outside, kept], axis=axis)
    kept = lax.slice_in_dim(cells, 1, size, axis=axis)
    return jnp.concatenate([kept, outside], axis=axis)


def lane_shifted(cells, step, outside):
    size = cells.shape[1]
    lanes = lax.broadcasted_iota(jnp.int32, cells.shape, 1)
    free = 0 if step > 0 else size - 1
    return jnp.where(lanes == free, outside, pltpu.roll(cells, step % size, axis=1))


def gather_kernel(
    sizes,
    partial_ref,
    vel_ref,
    vel_all,
    void_all,
    void_own,
    base_ref,
    parts,
    solid_all,
    my_edge,
    edge_lo,
    edge_hi,
    vel_lo,
    vel_hi,
    part_send,
    part_recv,
    vel_send,
    vel_recv,
    solid_send,
    solid_recv,
    edge_send,
    edge_recv,
    side_send,
    side_recv,
):
    size_x, size_y, size_z, bx, by = sizes
    owners = size_x * size_y
    row_count, lane_count = partial_ref.shape[1:]
    gx, gy, gz = (lax.axis_index(name) for name in ("gx", "gy", "gz"))
    me = gx * size_y + gy
    above, below = lax.rem(gz + 1, size_z), lax.rem(gz + size_z - 1, size_z)

    def at(owner, plane):
        return (owner // size_y, lax.rem(owner, size_y), plane)

    def slot(owner):
        return solid_all.at[owner // size_y + 1, lax.rem(owner, size_y) + 1]

    barrier = pltpu.get_barrier_semaphore()
    each(1, owners, lambda r: signal(barrier, at(lax.rem(me + r, owners), gz)))
    each(0, owners, lambda r: signal(barrier, at(lax.rem(me + r, owners), above)))
    each(0, owners, lambda r: signal(barrier, at(lax.rem(me + r, owners), below)))
    solid_all[...] = jnp.zeros_like(solid_all)
    pl.semaphore_wait(barrier, 3 * owners - 1)

    def part_copy(there, mine):
        return remote(
            partial_ref.at[there],
            parts.at[mine],
            part_send.at[there],
            part_recv.at[mine],
            at(there, gz),
        )

    def vel_copy(there, mine):
        return remote(
            vel_ref, vel_all.at[mine], vel_send.at[there], vel_recv.at[mine], at(there, gz)
        )

    def solid_copy(there, mine):
        return remote(
            slot(mine), slot(mine), solid_send.at[there], solid_recv.at[mine], at(there, gz)
        )

    def edge_copy(there, mine, side):
        return remote(
            my_edge,
            (edge_lo, edge_hi)[side].at[mine],
            edge_send.at[side, there],
            edge_recv.at[side, mine],
            at(there, (above, below)[side]),
        )

    sides = (
        remote(
            vel_ref.at[:, pl.ds(lane_count - 128, 128)],
            vel_lo,
            side_send.at[0],
            side_recv.at[0],
            (gx, gy, above),
        ),
        remote(
            vel_ref.at[:, pl.ds(0, 128)], vel_hi, side_send.at[1], side_recv.at[1], (gx, gy, below)
        ),
    )

    each(1, owners, lambda r: part_copy(lax.rem(me + r, owners), me).start())
    for copy in sides:
        copy.start()
    each(1, owners, lambda r: vel_copy(lax.rem(me + r, owners), me).start())
    vel_all[me] = vel_ref[...]

    def add_part(r, total):
        there = lax.rem(me + r, owners)
        part_copy(there, there).wait_recv()
        return total + parts[there]

    solid = lax.fori_loop(1, owners, add_part, partial_ref[me])
    rows_at = lax.broadcasted_iota(jnp.int32, (row_count, 128), 0)
    lanes_at = lax.broadcasted_iota(jnp.int32, (row_count, 128), 1)
    packed = [
        jnp.sum(jnp.where(rows_at == lanes_at, column, 0.0), axis=0, keepdims=True)
        for column in (solid[:, lane_count - 1 :], solid[:, :1])
    ]
    which = lax.broadcasted_iota(jnp.int32, (8, 128), 0)
    my_edge[...] = jnp.where(which == 0, packed[0], packed[1])
    slot(me)[...] = solid.reshape(bx, by, lane_count)
    each(1, owners, lambda r: solid_copy(lax.rem(me + r, owners), me).start())
    each(0, owners, lambda r: edge_copy(lax.rem(me + r, owners), me, 0).start())
    each(0, owners, lambda r: edge_copy(lax.rem(me + r, owners), me, 1).start())

    each(1, owners, lambda r: vel_copy(lax.rem(me + r, owners), lax.rem(me + r, owners)).wait_recv())
    for copy in sides:
        copy.wait_recv()
    own = vel_ref[...]
    own4 = own.reshape(3, bx, by, lane_count)

    def beside(owner, there):
        brick = vel_all[jnp.where(there, owner, me)].reshape(3, bx, by, lane_count)
        return jnp.where(there, brick, 0.0)

    x_before = beside(me - size_y, gx > 0)[:, bx - 1 :]
    x_after = beside(me + size_y, gx < size_x - 1)[:, :1]
    y_before = beside(me - 1, gy > 0)[:, :, by - 1 :]
    y_after = beside(me + 1, gy < size_y - 1)[:, :, :1]
    z_before = jnp.where(gz > 0, vel_lo[:, 127:], 0.0)
    z_after = jnp.where(gz < size_z - 1, vel_hi[:, :1], 0.0)
    total = shifted(own4, 1, -1, x_after) + shifted(own4, 1, 1, x_before)
    total = total + shifted(own4, 2, -1, y_after) + shifted(own4, 2, 1, y_before)
    total = total.reshape(3 * row_count, lane_count)
    total = total + lane_shifted(own, -1, z_after) + lane_shifted(own, 1, z_before)
    base_ref[...] = own + TIME_STEP * (total - 6.0 * own)

    each(1, owners, lambda r: solid_copy(lax.rem(me + r, owners), lax.rem(me + r, owners)).wait_recv())
    for side in range(2):
        each(0, owners, lambda r, side=side: edge_copy(r, r, side).wait_recv())

    def fill_brick(owner):
        ox, oy = owner // size_y + 1, lax.rem(owner, size_y) + 1
        cells = solid_all[ox, oy]
        flat = cells.reshape(row_count, lane_count)
        ends = []
        for refs, row, inside in ((edge_lo, 0, gz > 0), (edge_hi, 1, gz < size_z - 1)):
            line = refs[owner][row : row + 1]
            column = jnp.sum(jnp.where(rows_at == lanes_at, line, 0.0), axis=1, keepdims=True)
            ends.append(jnp.where(inside, column, 0.0))
        near = shifted(cells, 0, -1, solid_all[ox + 1, oy][:1])
        near = near + shifted(cells, 0, 1, solid_all[ox - 1, oy][bx - 1 :])
        near = near + shifted(cells, 1, -1, solid_all[ox, oy + 1][:, :1])
        near = near + shifted(cells, 1, 1, solid_all[ox, oy - 1][:, by - 1 :])
        near = near.reshape(row_count, lane_count)
        near = near + lane_shifted(flat, -1, ends[1]) + lane_shifted(flat, 1, ends[0])
        smooth = (flat + SPREAD * near) / (1.0 + 6 * SPREAD)
        void_all[owner] = jnp.maximum(1.0 - smooth, VOID_FLOOR)

    each(0, owners, fill_brick)
    void_own[...] = void_all[me]

    def end_sends(r):
        there = lax.rem(me + r, owners)
        part_copy(there, me).wait_send()
        vel_copy(there, me).wait_send()
        solid_copy(there, me).wait_send()

    each(1, owners, end_sends)
    for side in range(2):
        each(0, owners, lambda r, side=side: edge_copy(lax.rem(me + r, owners), me, side).wait_send())
    for copy in sides:
        copy.wait_send()


def source_kernel(sizes, part_ref, base_ref, void_ref, out_ref, parts, send_sem, recv_sem):
    size_x, size_y = sizes
    owners = size_x * size_y
    row_count = void_ref.shape[0]
    gx, gy, gz = (lax.axis_index(name) for name in ("gx", "gy", "gz"))
    me = gx * size_y + gy

    def at(owner):
        return (owner // size_y, lax.rem(owner, size_y), gz)

    barrier = pltpu.get_barrier_semaphore()
    each(1, owners, lambda r: signal(barrier, at(lax.rem(me + r, owners))))
    pl.semaphore_wait(barrier, owners - 1)

    def copy(there, mine):
        return remote(
            part_ref.at[there], parts.at[mine], send_sem.at[there], recv_sem.at[mine], at(there)
        )

    each(1, owners, lambda r: copy(lax.rem(me + r, owners), me).start())
    out_ref[...] = part_ref[me]

    def add(r):
        there = lax.rem(me + r, owners)
        copy(there, there).wait_recv()
        out_ref[...] += parts[there]

    each(1, owners, add)
    weight = TIME_STEP / (FLUID_DENSITY * void_ref[...])
    for comp in range(3):
        rows = pl.ds(comp * row_count, row_count)
        out_ref[rows, :] = base_ref[rows, :] - out_ref[rows, :] * weight
    each(1, owners, lambda r: copy(lax.rem(me + r, owners), me).wait_send())


def per_device(fluid_velocity, particle_velocity, diameter, particle_cell, block_owner):
    size_x, size_y, size_z = (lax.axis_size(name) for name in ("gx", "gy", "gz"))
    owners = size_x * size_y
    bx, by, lane_count = fluid_velocity.shape[1:]
    row_count = bx * by
    owner_list = block_owner[:, 0]
    vmem = pl.BlockSpec(memory_space=VMEM)
    smem = pl.BlockSpec(memory_space=SMEM)
    limit = 56 * 1024 * 1024

    def full(*shape):
        return jax.ShapeDtypeStruct(shape, jnp.float32)

    partial = pl.pallas_call(
        volume_kernel,
        out_shape=full(owners, row_count, lane_count),
        in_specs=[smem] + [vmem] * 2,
        out_specs=vmem,
        compiler_params=pltpu.CompilerParams(vmem_limit_bytes=limit),
        name="volume_deposit",
    )(owner_list, particle_cell, diameter)

    dma = pltpu.SemaphoreType.DMA
    vel_all, void_all, voidage, base = pl.pallas_call(
        functools.partial(gather_kernel, (size_x, size_y, size_z, bx, by)),
        out_shape=(
            full(owners, 3 * row_count, lane_count),
            full(owners, row_count, lane_count),
            full(row_count, lane_count),
            full(3 * row_count, lane_count),
        ),
        in_specs=[vmem] * 2,
        out_specs=(vmem,) * 4,
        scratch_shapes=[
            pltpu.VMEM((owners, row_count, lane_count), jnp.float32),
            pltpu.VMEM((size_x + 2, size_y + 2, bx, by, lane_count), jnp.float32),
            pltpu.VMEM((8, 128), jnp.float32),
            pltpu.VMEM((owners, 8, 128), jnp.float32),
            pltpu.VMEM((owners, 8, 128), jnp.float32),
            pltpu.VMEM((3 * row_count, 128), jnp.float32),
            pltpu.VMEM((3 * row_count, 128), jnp.float32),
        ]
        + [dma((owners,))] * 6
        + [dma((2, owners))] * 2
        + [dma((2,))] * 2,
        compiler_params=pltpu.CompilerParams(
            vmem_limit_bytes=limit, collective_id=0, has_side_effects=True
        ),
        name="gather_plane",
    )(partial, fluid_velocity.reshape(3 * row_count, lane_count))

    accel, force_part = pl.pallas_call(
        force_kernel,
        out_shape=(
            jax.ShapeDtypeStruct(particle_velocity.shape, jnp.float32),
            full(owners, 3 * row_count, lane_count),
        ),
        in_specs=[smem] + [vmem] * 5,
        out_specs=(vmem,) * 2,
        scratch_shapes=[pltpu.VMEM((owners, 8 * row_count, lane_count), jnp.bfloat16)],
        compiler_params=pltpu.CompilerParams(vmem_limit_bytes=limit),
        name="force_deposit",
    )(owner_list, particle_cell, diameter, particle_velocity, vel_all, void_all)

    fluid_next = pl.pallas_call(
        functools.partial(source_kernel, (size_x, size_y)),
        out_shape=full(3 * row_count, lane_count),
        in_specs=[vmem] * 3,
        out_specs=vmem,
        scratch_shapes=[
            pltpu.VMEM((owners, 3 * row_count, lane_count), jnp.float32),
            dma((owners,)),
            dma((owners,)),
        ],
        compiler_params=pltpu.CompilerParams(
            vmem_limit_bytes=limit, collective_id=1, has_side_effects=True
        ),
        name="sum_source",
    )(force_part, base, voidage)
    return (
        accel,
        voidage.reshape(bx, by, lane_count),
        fluid_next.reshape(3, bx, by, lane_count),
    )


def solution(mesh):
    placed = (
        P(None, "gx", "gy", "gz"),
        P(("gx", "gy", "gz"), None, None),
        P(("gx", "gy", "gz"), None),
        P(("gx", "gy", "gz"), None),
        P(("gx", "gy", "gz"), None),
    )
    return jax.shard_map(
        per_device,
        mesh=mesh,
        in_specs=placed,
        out_specs=(
            P(("gx", "gy", "gz"), None, None),
            P("gx", "gy", "gz"),
            P(None, "gx", "gy", "gz"),
        ),
        check_vma=False,
    )
```

```python
import functools
import math

import jax
import jax.numpy as jnp
from jax import lax
from jax.experimental import pallas as pl
from jax.experimental.pallas import tpu as pltpu
from jax.sharding import PartitionSpec as P

VISCOSITY = 0.1
FLUID_DENSITY = 0.05
SOLID_DENSITY = 2.5
TIME_STEP = 0.05
VOID_FLOOR = 0.35
SPREAD = 0.1
GROUP = 8
PLANE = ("gx", "gy")
VMEM = pltpu.MemorySpace.VMEM
SMEM = pltpu.MemorySpace.SMEM


def halves(value):
    high = value.astype(jnp.bfloat16)
    low = (value - high.astype(jnp.float32)).astype(jnp.bfloat16)
    return high, low


def lane_onehot(cell_row, lane_count, per_block):
    lanes = lax.broadcasted_iota(jnp.int32, (lane_count, per_block), 0)
    hit = lanes == (cell_row & (lane_count - 1))
    return jnp.where(hit, 1.0, 0.0).astype(jnp.bfloat16)


def row_hits(cell_row, row_count, lane_count, per_block):
    rows = lax.broadcasted_iota(jnp.int32, (row_count, per_block), 0)
    return rows == lax.shift_right_logical(cell_row, lane_count.bit_length() - 1)


def spread_rows(hits, values):
    pieces = [halves(value) for value in values]
    stacked = [jnp.where(hits, part[0].astype(jnp.float32), 0.0) for part in pieces]
    stacked += [jnp.where(hits, part[1].astype(jnp.float32), 0.0) for part in pieces]
    return jnp.concatenate(stacked, axis=0).astype(jnp.bfloat16)


def onto_cells(rows, lane_hot):
    both = lax.dot_general(
        rows, lane_hot, (((1,), (1,)), ((), ())), preferred_element_type=jnp.float32
    )
    half = both.shape[0] // 2
    return both[:half] + both[half:]


def deposit_volume(owner_ref, cell_ref, diam_ref, out_ref):
    blocks, per_block = cell_ref.shape
    owners, row_count, lane_count = out_ref.shape
    dense = GROUP * row_count
    shift = lane_count.bit_length() - 1
    out_ref[...] = jnp.zeros_like(out_ref)

    def step(index):
        group, bunch = index // (owners // GROUP), lax.rem(index, owners // GROUP)
        start = pl.multiple_of(group * GROUP, GROUP)
        cells = cell_ref[pl.ds(start, GROUP), :]
        diam = diam_ref[pl.ds(start, GROUP), :]
        volume = math.pi / 6 * diam * diam * diam
        ids = lax.broadcasted_iota(jnp.int32, (dense, per_block), 0) + bunch * dense
        rows, hots = [], []
        for i in range(GROUP):
            row = cells[i : i + 1]
            at = owner_ref[start + i] * row_count + lax.shift_right_logical(row, shift)
            rows.append(spread_rows(ids == at, [volume[i : i + 1]]))
            hots.append(lane_onehot(row, lane_count, per_block))
        add = onto_cells(jnp.concatenate(rows, axis=1), jnp.concatenate(hots, axis=1))
        into = pl.ds(bunch * GROUP, GROUP)
        out_ref[into] = out_ref[into] + add.reshape(GROUP, row_count, lane_count)

    each(0, (blocks // GROUP) * (owners // GROUP), step)


def force_kernel(
    owner_ref, cell_ref, diam_ref, part_ref, vel_ref, void_ref, accel_ref, out_ref, table
):
    blocks, per_block = cell_ref.shape
    owners, row_count, lane_count = void_ref.shape
    out_ref[...] = jnp.zeros_like(out_ref)

    @pl.loop(0, owners)
    def _(owner):
        both = jnp.concatenate([vel_ref[owner], void_ref[owner]], axis=0)
        high, low = halves(both)
        table[owner] = jnp.concatenate([high, low], axis=0)

    @pl.loop(0, blocks // GROUP)
    def _(group):
        start = pl.multiple_of(group * GROUP, GROUP)
        cells = cell_ref[pl.ds(start, GROUP), :]
        diam = diam_ref[pl.ds(start, GROUP), :]
        hots, hit_list, looked = [], [], [[], [], [], []]
        for i in range(GROUP):
            row = cells[i : i + 1]
            hot = lane_onehot(row, lane_count, per_block)
            hits = row_hits(row, row_count, lane_count, per_block)
            hots.append(hot)
            hit_list.append(hits)
            both = jnp.dot(
                table[owner_ref[start + i]], hot, preferred_element_type=jnp.float32
            )
            half = both.shape[0] // 2
            both = both[:half] + both[half:]
            for comp in range(4):
                piece = both[comp * row_count : (comp + 1) * row_count]
                looked[comp].append(
                    jnp.sum(jnp.where(hits, piece, 0.0), axis=0, keepdims=True)
                )
        at = [jnp.concatenate(rows, axis=0) for rows in looked]
        slip = [at[comp] - part_ref[comp, pl.ds(start, GROUP), :] for comp in range(3)]
        void_at = at[3]
        speed = jnp.sqrt(slip[0] * slip[0] + slip[1] * slip[1] + slip[2] * slip[2])
        reynolds = jnp.maximum(void_at * diam * speed / VISCOSITY, 1.0)
        drag_coeff = 0.63 + 4.8 / jnp.sqrt(reynolds)
        drag_coeff = drag_coeff * drag_coeff
        gap = 1.5 - jnp.log(reynolds) * (1.0 / math.log(10.0))
        chi_exp = 3.7 - 0.65 * jnp.exp(-0.5 * gap * gap)
        magnitude = 0.5 * drag_coeff * FLUID_DENSITY * (math.pi / 4) * diam * diam
        magnitude = magnitude * jnp.exp((2.0 - chi_exp) * jnp.log(void_at)) * speed
        force = [magnitude * slip[comp] for comp in range(3)]
        mass = SOLID_DENSITY * (math.pi / 6 * diam * diam * diam)
        for comp in range(3):
            accel_ref[comp, pl.ds(start, GROUP), :] = force[comp] / mass
        adds = []
        for i in range(GROUP):
            rows = spread_rows(hit_list[i], [force[comp][i : i + 1] for comp in range(3)])
            adds.append(onto_cells(rows, hots[i]))
        for i in range(GROUP):
            owner = owner_ref[start + i]
            out_ref[owner] = out_ref[owner] + adds[i]


def each(first, last, body):
    def step(i, carry):
        body(i)
        return carry

    lax.fori_loop(first, last, step, 0)


def remote(src, dst, send_sem, recv_sem, device):
    return pltpu.make_async_remote_copy(
        src_ref=src,
        dst_ref=dst,
        send_sem=send_sem,
        recv_sem=recv_sem,
        device_id=device,
        device_id_type=pl.DeviceIdType.MESH,
    )


def signal(semaphore, device):
    pl.semaphore_signal(
        semaphore, inc=1, device_id=device, device_id_type=pl.DeviceIdType.MESH
    )


def shifted(cells, axis, step, outside):
    size = cells.shape[axis]
    if step > 0:
        kept = lax.slice_in_dim(cells, 0, size - 1, axis=axis)
        return jnp.concatenate([outside, kept], axis=axis)
    kept = lax.slice_in_dim(cells, 1, size, axis=axis)
    return jnp.concatenate([kept, outside], axis=axis)


def lane_shifted(cells, step, outside):
    size = cells.shape[1]
    lanes = lax.broadcasted_iota(jnp.int32, cells.shape, 1)
    free = 0 if step > 0 else size - 1
    return jnp.where(lanes == free, outside, pltpu.roll(cells, step % size, axis=1))


class Plane:
    def __init__(self, size_x, size_y):
        self.size_x, self.size_y = size_x, size_y
        self.gx, self.gy, self.gz = (lax.axis_index(name) for name in ("gx", "gy", "gz"))
        self.me = self.owner(self.gx, self.gy)

    def owner(self, x, y):
        return x * self.size_y + y

    def others_x(self, body):
        each(1, self.size_x, lambda r: body(lax.rem(self.gx + r, self.size_x)))

    def others_y(self, body):
        each(1, self.size_y, lambda r: body(lax.rem(self.gy + r, self.size_y)))

    def greet(self, barrier):
        self.others_x(lambda x: signal(barrier, (x, self.gy, self.gz)))
        self.others_y(lambda y: signal(barrier, (self.gx, y, self.gz)))
        return self.size_x + self.size_y - 2


class Gather:
    def __init__(self, plane, source, slot, send_x, send_y, recv):
        self.plane, self.source, self.slot = plane, source, slot
        self.send_x, self.send_y, self.recv = send_x, send_y, recv

    def along_x(self, x, owner):
        p = self.plane
        return remote(
            self.source,
            self.slot(owner),
            self.send_x.at[x],
            self.recv.at[owner],
            (x, p.gy, p.gz),
        )

    def along_y(self, x, y, owner):
        p = self.plane
        return remote(
            self.slot(owner),
            self.slot(owner),
            self.send_y.at[y, x],
            self.recv.at[owner],
            (p.gx, y, p.gz),
        )

    def start(self):
        p = self.plane
        p.others_x(lambda x: self.along_x(x, p.me).start())
        p.others_y(lambda y: self.along_y(p.gx, y, p.me).start())

    def forward(self):
        p = self.plane

        def pass_on(x):
            owner = p.owner(x, p.gy)
            self.along_x(x, owner).wait_recv()
            p.others_y(lambda y: self.along_y(x, y, owner).start())

        p.others_x(pass_on)

    def wait(self):
        p = self.plane

        def arrive(y):
            def one(r):
                x = lax.rem(p.gx + r, p.size_x)
                self.along_y(x, y, p.owner(x, y)).wait_recv()

            each(0, p.size_x, one)

        p.others_y(arrive)

    def finish(self):
        p = self.plane
        p.others_x(lambda x: self.along_x(x, p.me).wait_send())

        def one(x):
            p.others_y(lambda y: self.along_y(x, y, p.owner(x, p.gy)).wait_send())

        each(0, p.size_x, one)


class Scatter:
    def __init__(self, plane, source, first, middle, last, send_y, recv_y, send_x, recv_x):
        self.plane, self.source = plane, source
        self.first, self.middle, self.last = first, middle, last
        self.send_y, self.recv_y, self.send_x, self.recv_x = send_y, recv_y, send_x, recv_x

    def along_y(self, x, y, mine):
        p = self.plane
        return remote(
            self.source.at[p.owner(x, y)],
            self.first.at[mine, x],
            self.send_y.at[y, x],
            self.recv_y.at[mine, x],
            (p.gx, y, p.gz),
        )

    def along_x(self, x, mine):
        p = self.plane
        return remote(
            self.middle.at[x],
            self.last.at[mine],
            self.send_x.at[x],
            self.recv_x.at[mine],
            (x, p.gy, p.gz),
        )

    def start(self):
        p = self.plane

        def one(x):
            p.others_y(lambda y: self.along_y(x, y, p.gy).start())

        p.others_x(one)
        one(p.gx)

    def forward(self):
        p = self.plane

        def one(x):
            self.middle[x] = self.source[p.owner(x, p.gy)]

            def add(y):
                self.along_y(x, y, y).wait_recv()
                self.middle[x] = self.middle[x] + self.first[y, x]

            p.others_y(add)

        def send(x):
            one(x)
            self.along_x(x, p.gx).start()

        p.others_x(send)
        one(p.gx)

    def total(self, out_ref):
        p = self.plane
        out_ref[...] = self.middle[p.gx]

        def add(x):
            self.along_x(x, x).wait_recv()
            out_ref[...] = out_ref[...] + self.last[x]

        p.others_x(add)

    def finish(self):
        p = self.plane

        def one(x):
            p.others_y(lambda y: self.along_y(x, y, p.gy).wait_send())

        each(0, p.size_x, one)
        p.others_x(lambda x: self.along_x(x, p.gx).wait_send())


def gather_sems(size_x, size_y):
    dma = pltpu.SemaphoreType.DMA
    return [dma((size_x,)), dma((size_y, size_x)), dma((size_x * size_y,))]


def scatter_scratch(size_x, size_y, rows, lanes):
    dma = pltpu.SemaphoreType.DMA
    return [
        pltpu.VMEM((size_y, size_x, rows, lanes), jnp.float32),
        pltpu.VMEM((size_x, rows, lanes), jnp.float32),
        pltpu.VMEM((size_x, rows, lanes), jnp.float32),
        dma((size_y, size_x)),
        dma((size_y, size_x)),
        dma((size_x,)),
        dma((size_x,)),
    ]


def gather_kernel(
    sizes,
    owner_ref,
    cell_ref,
    diam_ref,
    vel_ref,
    vel_all,
    void_all,
    void_own,
    base_ref,
    partial_ref,
    solid_ref,
    solid_all,
    my_edge,
    edges,
    vel_lo,
    vel_hi,
    edge_send,
    edge_recv,
    side_send,
    side_recv,
    *rest,
):
    size_x, size_y, size_z, bx, by = sizes
    owners = size_x * size_y
    row_count, lane_count = partial_ref.shape[1:]
    plane = Plane(size_x, size_y)
    gx, gy, gz, me = plane.gx, plane.gy, plane.gz, plane.me
    above, below = lax.rem(gz + 1, size_z), lax.rem(gz + size_z - 1, size_z)

    def slot(owner):
        return solid_all.at[owner // size_y + 1, lax.rem(owner, size_y) + 1]

    def place(r, other):
        owner = lax.rem(me + r, owners)
        return (owner // size_y, lax.rem(owner, size_y), other)

    barrier = pltpu.get_barrier_semaphore()
    greeted = plane.greet(barrier)
    each(0, owners, lambda r: signal(barrier, place(r, above)))
    each(0, owners, lambda r: signal(barrier, place(r, below)))
    solid_all[...] = jnp.zeros_like(solid_all)
    vel_all[me] = vel_ref[...]
    pl.semaphore_wait(barrier, greeted + 2 * owners)

    vel = Gather(plane, vel_ref, lambda owner: vel_all.at[owner], *rest[:3])
    solid_gather = Gather(plane, slot(me), slot, *rest[3:6])
    scatter = Scatter(plane, partial_ref, *rest[6:])

    def edge_copy(r, mine, side):
        there = lax.rem(me + r, owners)
        return remote(
            my_edge.at[side],
            edges.at[side, mine],
            edge_send.at[side, there],
            edge_recv.at[side, mine],
            place(r, (above, below)[side]),
        )

    sides = (
        remote(
            vel_ref.at[:, pl.ds(lane_count - 128, 128)],
            vel_lo,
            side_send.at[0],
            side_recv.at[0],
            (gx, gy, above),
        ),
        remote(
            vel_ref.at[:, pl.ds(0, 128)], vel_hi, side_send.at[1], side_recv.at[1], (gx, gy, below)
        ),
    )
    vel.start()
    for copy in sides:
        copy.start()
    deposit_volume(owner_ref, cell_ref, diam_ref, partial_ref)
    scatter.start()
    scatter.forward()
    vel.forward()
    scatter.total(solid_ref)
    solid = solid_ref[...]
    slot(me)[...] = solid.reshape(bx, by, lane_count)
    solid_gather.start()
    rows_at = lax.broadcasted_iota(jnp.int32, (row_count, 128), 0)
    lanes_at = lax.broadcasted_iota(jnp.int32, (row_count, 128), 1)
    for side, column in enumerate((solid[:, lane_count - 1 :], solid[:, :1])):
        my_edge[side] = jnp.sum(
            jnp.where(rows_at == lanes_at, column, 0.0), axis=0, keepdims=True
        )
        each(0, owners, lambda r, side=side: edge_copy(r, me, side).start())
    solid_gather.forward()

    vel.wait()
    for copy in sides:
        copy.wait_recv()
    own = vel_ref[...]
    own4 = own.reshape(3, bx, by, lane_count)

    def beside(owner, there):
        brick = vel_all[jnp.where(there, owner, me)].reshape(3, bx, by, lane_count)
        return jnp.where(there, brick, 0.0)

    x_before = beside(me - size_y, gx > 0)[:, bx - 1 :]
    x_after = beside(me + size_y, gx < size_x - 1)[:, :1]
    y_before = beside(me - 1, gy > 0)[:, :, by - 1 :]
    y_after = beside(me + 1, gy < size_y - 1)[:, :, :1]
    z_before = jnp.where(gz > 0, vel_lo[:, 127:], 0.0)
    z_after = jnp.where(gz < size_z - 1, vel_hi[:, :1], 0.0)
    total = shifted(own4, 1, -1, x_after) + shifted(own4, 1, 1, x_before)
    total = total + shifted(own4, 2, -1, y_after) + shifted(own4, 2, 1, y_before)
    total = total.reshape(3 * row_count, lane_count)
    total = total + lane_shifted(own, -1, z_after) + lane_shifted(own, 1, z_before)
    base_ref[...] = own + TIME_STEP * (total - 6.0 * own)

    solid_gather.wait()
    for side in range(2):
        each(0, owners, lambda r, side=side: edge_copy(0, r, side).wait_recv())

    def fill_brick(owner):
        ox, oy = owner // size_y + 1, lax.rem(owner, size_y) + 1
        cells = solid_all[ox, oy]
        flat = cells.reshape(row_count, lane_count)
        ends = []
        for side, inside in ((0, gz > 0), (1, gz < size_z - 1)):
            line = edges[side, owner]
            column = jnp.sum(jnp.where(rows_at == lanes_at, line, 0.0), axis=1, keepdims=True)
            ends.append(jnp.where(inside, column, 0.0))
        near = shifted(cells, 0, -1, solid_all[ox + 1, oy][:1])
        near = near + shifted(cells, 0, 1, solid_all[ox - 1, oy][bx - 1 :])
        near = near + shifted(cells, 1, -1, solid_all[ox, oy + 1][:, :1])
        near = near + shifted(cells, 1, 1, solid_all[ox, oy - 1][:, by - 1 :])
        near = near.reshape(row_count, lane_count)
        near = near + lane_shifted(flat, -1, ends[1]) + lane_shifted(flat, 1, ends[0])
        smooth = (flat + SPREAD * near) / (1.0 + 6 * SPREAD)
        void_all[owner] = jnp.maximum(1.0 - smooth, VOID_FLOOR)

    each(0, owners, fill_brick)
    void_own[...] = void_all[me]

    for copy in sides:
        copy.wait_send()
    for side in range(2):
        each(0, owners, lambda r, side=side: edge_copy(r, me, side).wait_send())
    vel.finish()
    scatter.finish()
    solid_gather.finish()


def source_kernel(sizes, part_ref, base_ref, void_ref, out_ref, *rest):
    row_count = void_ref.shape[0]
    plane = Plane(*sizes)
    barrier = pltpu.get_barrier_semaphore()
    pl.semaphore_wait(barrier, plane.greet(barrier))
    scatter = Scatter(plane, part_ref, *rest)
    scatter.start()
    scatter.forward()
    scatter.total(out_ref)
    weight = TIME_STEP / (FLUID_DENSITY * void_ref[...])
    for comp in range(3):
        rows = pl.ds(comp * row_count, row_count)
        out_ref[rows, :] = base_ref[rows, :] - out_ref[rows, :] * weight
    scatter.finish()


def per_device(fluid_velocity, particle_velocity, diameter, particle_cell, block_owner):
    size_x, size_y, size_z = (lax.axis_size(name) for name in ("gx", "gy", "gz"))
    owners = size_x * size_y
    bx, by, lane_count = fluid_velocity.shape[1:]
    row_count = bx * by
    owner_list = block_owner[:, 0]
    vmem = pl.BlockSpec(memory_space=VMEM)
    smem = pl.BlockSpec(memory_space=SMEM)
    limit = 56 * 1024 * 1024

    def full(*shape):
        return jax.ShapeDtypeStruct(shape, jnp.float32)

    dma = pltpu.SemaphoreType.DMA
    vel_all, void_all, voidage, base = pl.pallas_call(
        functools.partial(gather_kernel, (size_x, size_y, size_z, bx, by)),
        out_shape=(
            full(owners, 3 * row_count, lane_count),
            full(owners, row_count, lane_count),
            full(row_count, lane_count),
            full(3 * row_count, lane_count),
        ),
        in_specs=[smem] + [vmem] * 3,
        out_specs=(vmem,) * 4,
        scratch_shapes=[
            pltpu.VMEM((owners, row_count, lane_count), jnp.float32),
            pltpu.VMEM((row_count, lane_count), jnp.float32),
            pltpu.VMEM((size_x + 2, size_y + 2, bx, by, lane_count), jnp.float32),
            pltpu.VMEM((2, 1, 128), jnp.float32),
            pltpu.VMEM((2, owners, 1, 128), jnp.float32),
            pltpu.VMEM((3 * row_count, 128), jnp.float32),
            pltpu.VMEM((3 * row_count, 128), jnp.float32),
            dma((2, owners)),
            dma((2, owners)),
            dma((2,)),
            dma((2,)),
        ]
        + gather_sems(size_x, size_y) * 2
        + scatter_scratch(size_x, size_y, row_count, lane_count),
        compiler_params=pltpu.CompilerParams(
            vmem_limit_bytes=limit, collective_id=0, has_side_effects=True
        ),
        name="gather_plane",
    )(
        owner_list,
        particle_cell,
        diameter,
        fluid_velocity.reshape(3 * row_count, lane_count),
    )

    accel, force_part = pl.pallas_call(
        force_kernel,
        out_shape=(
            full(3, *diameter.shape),
            full(owners, 3 * row_count, lane_count),
        ),
        in_specs=[smem] + [vmem] * 5,
        out_specs=(vmem,) * 2,
        scratch_shapes=[pltpu.VMEM((owners, 8 * row_count, lane_count), jnp.bfloat16)],
        compiler_params=pltpu.CompilerParams(vmem_limit_bytes=limit),
        name="force_deposit",
    )(owner_list, particle_cell, diameter, particle_velocity.transpose(1, 0, 2), vel_all, void_all)

    fluid_next = pl.pallas_call(
        functools.partial(source_kernel, (size_x, size_y)),
        out_shape=full(3 * row_count, lane_count),
        in_specs=[vmem] * 3,
        out_specs=vmem,
        scratch_shapes=scatter_scratch(size_x, size_y, 3 * row_count, lane_count),
        compiler_params=pltpu.CompilerParams(
            vmem_limit_bytes=limit, collective_id=1, has_side_effects=True
        ),
        name="sum_source",
    )(force_part, base, voidage)
    return (
        accel.transpose(1, 0, 2),
        voidage.reshape(bx, by, lane_count),
        fluid_next.reshape(3, bx, by, lane_count),
    )


def solution(mesh):
    placed = (
        P(None, "gx", "gy", "gz"),
        P(("gx", "gy", "gz"), None, None),
        P(("gx", "gy", "gz"), None),
        P(("gx", "gy", "gz"), None),
        P(("gx", "gy", "gz"), None),
    )
    return jax.shard_map(
        per_device,
        mesh=mesh,
        in_specs=placed,
        out_specs=(
            P(("gx", "gy", "gz"), None, None),
            P("gx", "gy", "gz"),
            P(None, "gx", "gy", "gz"),
        ),
        check_vma=False,
    )
```

```python
import functools
import math

import jax
import jax.numpy as jnp
from jax import lax
from jax.experimental import pallas as pl
from jax.experimental.pallas import tpu as pltpu
from jax.sharding import PartitionSpec as P

VISCOSITY = 0.1
FLUID_DENSITY = 0.05
SOLID_DENSITY = 2.5
TIME_STEP = 0.05
VOID_FLOOR = 0.35
SPREAD = 0.1
GROUP = 8
PLANE = ("gx", "gy")
VMEM = pltpu.MemorySpace.VMEM
SMEM = pltpu.MemorySpace.SMEM


def halves(value):
    high = value.astype(jnp.bfloat16)
    low = (value - high.astype(jnp.float32)).astype(jnp.bfloat16)
    return high, low


def lane_onehot(cell_row, lane_count, per_block):
    lanes = lax.broadcasted_iota(jnp.int32, (lane_count, per_block), 0)
    hit = lanes == (cell_row & (lane_count - 1))
    return jnp.where(hit, 1.0, 0.0).astype(jnp.bfloat16)


def row_hits(cell_row, row_count, lane_count, per_block):
    rows = lax.broadcasted_iota(jnp.int32, (row_count, per_block), 0)
    return rows == lax.shift_right_logical(cell_row, lane_count.bit_length() - 1)


def spread_rows(hits, values):
    pieces = [halves(value) for value in values]
    stacked = [jnp.where(hits, part[0].astype(jnp.float32), 0.0) for part in pieces]
    stacked += [jnp.where(hits, part[1].astype(jnp.float32), 0.0) for part in pieces]
    return jnp.concatenate(stacked, axis=0).astype(jnp.bfloat16)


def onto_cells(rows, lane_hot):
    both = lax.dot_general(
        rows, lane_hot, (((1,), (1,)), ((), ())), preferred_element_type=jnp.float32
    )
    half = both.shape[0] // 2
    return both[:half] + both[half:]


def deposit_volume(owner_ref, cell_ref, diam_ref, out_ref):
    blocks, per_block = cell_ref.shape
    owners, row_count, lane_count = out_ref.shape
    dense = GROUP * row_count
    shift = lane_count.bit_length() - 1
    out_ref[...] = jnp.zeros_like(out_ref)

    def step(index):
        group, bunch = index // (owners // GROUP), lax.rem(index, owners // GROUP)
        start = pl.multiple_of(group * GROUP, GROUP)
        cells = cell_ref[pl.ds(start, GROUP), :]
        diam = diam_ref[pl.ds(start, GROUP), :]
        volume = math.pi / 6 * diam * diam * diam
        ids = lax.broadcasted_iota(jnp.int32, (dense, per_block), 0) + bunch * dense
        rows, hots = [], []
        for i in range(GROUP):
            row = cells[i : i + 1]
            at = owner_ref[start + i] * row_count + lax.shift_right_logical(row, shift)
            rows.append(spread_rows(ids == at, [volume[i : i + 1]]))
            hots.append(lane_onehot(row, lane_count, per_block))
        add = onto_cells(jnp.concatenate(rows, axis=1), jnp.concatenate(hots, axis=1))
        into = pl.ds(bunch * GROUP, GROUP)
        out_ref[into] = out_ref[into] + add.reshape(GROUP, row_count, lane_count)

    each(0, (blocks // GROUP) * (owners // GROUP), step)


def force_kernel(
    owner_ref,
    cell_ref,
    diam_ref,
    part_ref,
    vel_ref,
    void_ref,
    own_ref,
    accel_ref,
    out_ref,
    void_out,
    table,
):
    blocks, per_block = cell_ref.shape
    owners, row_count, lane_count = void_ref.shape
    out_ref[...] = jnp.zeros_like(out_ref)
    void_out[...] = own_ref[...]

    @pl.loop(0, owners)
    def _(owner):
        both = jnp.concatenate([vel_ref[owner], void_ref[owner]], axis=0)
        high, low = halves(both)
        table[owner] = jnp.concatenate([high, low], axis=0)

    @pl.loop(0, blocks // GROUP)
    def _(group):
        start = pl.multiple_of(group * GROUP, GROUP)
        cells = cell_ref[pl.ds(start, GROUP), :]
        diam = diam_ref[pl.ds(start, GROUP), :]
        hots, hit_list, looked = [], [], [[], [], [], []]
        for i in range(GROUP):
            row = cells[i : i + 1]
            hot = lane_onehot(row, lane_count, per_block)
            hits = row_hits(row, row_count, lane_count, per_block)
            hots.append(hot)
            hit_list.append(hits)
            both = jnp.dot(
                table[owner_ref[start + i]], hot, preferred_element_type=jnp.float32
            )
            half = both.shape[0] // 2
            both = both[:half] + both[half:]
            for comp in range(4):
                piece = both[comp * row_count : (comp + 1) * row_count]
                looked[comp].append(
                    jnp.sum(jnp.where(hits, piece, 0.0), axis=0, keepdims=True)
                )
        at = [jnp.concatenate(rows, axis=0) for rows in looked]
        slip = [at[comp] - part_ref[comp, pl.ds(start, GROUP), :] for comp in range(3)]
        void_at = at[3]
        speed = jnp.sqrt(slip[0] * slip[0] + slip[1] * slip[1] + slip[2] * slip[2])
        reynolds = jnp.maximum(void_at * diam * speed / VISCOSITY, 1.0)
        drag_coeff = 0.63 + 4.8 / jnp.sqrt(reynolds)
        drag_coeff = drag_coeff * drag_coeff
        gap = 1.5 - jnp.log(reynolds) * (1.0 / math.log(10.0))
        chi_exp = 3.7 - 0.65 * jnp.exp(-0.5 * gap * gap)
        magnitude = 0.5 * drag_coeff * FLUID_DENSITY * (math.pi / 4) * diam * diam
        magnitude = magnitude * jnp.exp((2.0 - chi_exp) * jnp.log(void_at)) * speed
        force = [magnitude * slip[comp] for comp in range(3)]
        mass = SOLID_DENSITY * (math.pi / 6 * diam * diam * diam)
        for comp in range(3):
            accel_ref[comp, pl.ds(start, GROUP), :] = force[comp] / mass
        adds = []
        for i in range(GROUP):
            rows = spread_rows(hit_list[i], [force[comp][i : i + 1] for comp in range(3)])
            adds.append(onto_cells(rows, hots[i]))
        for i in range(GROUP):
            owner = owner_ref[start + i]
            out_ref[owner] = out_ref[owner] + adds[i]


def each(first, last, body):
    def step(i, carry):
        body(i)
        return carry

    lax.fori_loop(first, last, step, 0)


def remote(src, dst, send_sem, recv_sem, device):
    return pltpu.make_async_remote_copy(
        src_ref=src,
        dst_ref=dst,
        send_sem=send_sem,
        recv_sem=recv_sem,
        device_id=device,
        device_id_type=pl.DeviceIdType.MESH,
    )


def signal(semaphore, device):
    pl.semaphore_signal(
        semaphore, inc=1, device_id=device, device_id_type=pl.DeviceIdType.MESH
    )


def shifted(cells, axis, step, outside):
    size = cells.shape[axis]
    if step > 0:
        kept = lax.slice_in_dim(cells, 0, size - 1, axis=axis)
        return jnp.concatenate([outside, kept], axis=axis)
    kept = lax.slice_in_dim(cells, 1, size, axis=axis)
    return jnp.concatenate([kept, outside], axis=axis)


def lane_shifted(cells, step, outside):
    size = cells.shape[1]
    lanes = lax.broadcasted_iota(jnp.int32, cells.shape, 1)
    free = 0 if step > 0 else size - 1
    return jnp.where(lanes == free, outside, pltpu.roll(cells, step % size, axis=1))


class Plane:
    def __init__(self, size_x, size_y):
        self.size_x, self.size_y = size_x, size_y
        self.gx, self.gy, self.gz = (lax.axis_index(name) for name in ("gx", "gy", "gz"))
        self.me = self.owner(self.gx, self.gy)

    def owner(self, x, y):
        return x * self.size_y + y

    def others_x(self, body):
        each(1, self.size_x, lambda r: body(lax.rem(self.gx + r, self.size_x)))

    def others_y(self, body):
        each(1, self.size_y, lambda r: body(lax.rem(self.gy + r, self.size_y)))

    def greet(self, barrier):
        self.others_x(lambda x: signal(barrier, (x, self.gy, self.gz)))
        self.others_y(lambda y: signal(barrier, (self.gx, y, self.gz)))
        return self.size_x + self.size_y - 2


class Gather:
    def __init__(self, plane, source, slot, send_x, send_y, recv):
        self.plane, self.source, self.slot = plane, source, slot
        self.send_x, self.send_y, self.recv = send_x, send_y, recv

    def along_x(self, x, owner):
        p = self.plane
        return remote(
            self.source,
            self.slot(owner),
            self.send_x.at[x],
            self.recv.at[owner],
            (x, p.gy, p.gz),
        )

    def along_y(self, x, y, owner):
        p = self.plane
        return remote(
            self.slot(owner),
            self.slot(owner),
            self.send_y.at[y, x],
            self.recv.at[owner],
            (p.gx, y, p.gz),
        )

    def start(self):
        p = self.plane
        p.others_x(lambda x: self.along_x(x, p.me).start())
        p.others_y(lambda y: self.along_y(p.gx, y, p.me).start())

    def forward(self, first, last):
        p = self.plane

        def pass_on(r):
            x = lax.rem(p.gx + p.size_x - r, p.size_x)
            owner = p.owner(x, p.gy)
            self.along_x(x, owner).wait_recv()
            p.others_y(lambda y: self.along_y(x, y, owner).start())

        each(first, last, pass_on)

    def wait(self):
        p = self.plane

        def arrive(y):
            def one(r):
                x = lax.rem(p.gx + r, p.size_x)
                self.along_y(x, y, p.owner(x, y)).wait_recv()

            each(0, p.size_x, one)

        p.others_y(arrive)

    def finish(self):
        p = self.plane
        p.others_x(lambda x: self.along_x(x, p.me).wait_send())

        def one(x):
            p.others_y(lambda y: self.along_y(x, y, p.owner(x, p.gy)).wait_send())

        each(0, p.size_x, one)


class Scatter:
    def __init__(self, plane, source, first, middle, last, send_y, recv_y, send_x, recv_x):
        self.plane, self.source = plane, source
        self.first, self.middle, self.last = first, middle, last
        self.send_y, self.recv_y, self.send_x, self.recv_x = send_y, recv_y, send_x, recv_x

    def along_y(self, x, y, mine):
        p = self.plane
        return remote(
            self.source.at[p.owner(x, y)],
            self.first.at[mine, x],
            self.send_y.at[y, x],
            self.recv_y.at[mine, x],
            (p.gx, y, p.gz),
        )

    def along_x(self, x, mine):
        p = self.plane
        return remote(
            self.middle.at[x],
            self.last.at[mine],
            self.send_x.at[x],
            self.recv_x.at[mine],
            (x, p.gy, p.gz),
        )

    def start(self):
        p = self.plane

        def one(x):
            p.others_y(lambda y: self.along_y(x, y, p.gy).start())

        p.others_x(one)
        one(p.gx)

    def forward(self):
        p = self.plane

        def one(x):
            self.middle[x] = self.source[p.owner(x, p.gy)]

            def add(y):
                self.along_y(x, y, y).wait_recv()
                self.middle[x] = self.middle[x] + self.first[y, x]

            p.others_y(add)

        def send(x):
            one(x)
            self.along_x(x, p.gx).start()

        p.others_x(send)
        one(p.gx)

    def total(self, out_ref):
        p = self.plane
        out_ref[...] = self.middle[p.gx]

        def add(x):
            self.along_x(x, x).wait_recv()
            out_ref[...] = out_ref[...] + self.last[x]

        p.others_x(add)

    def finish(self):
        p = self.plane

        def one(x):
            p.others_y(lambda y: self.along_y(x, y, p.gy).wait_send())

        each(0, p.size_x, one)
        p.others_x(lambda x: self.along_x(x, p.gx).wait_send())


def gather_sems(size_x, size_y):
    dma = pltpu.SemaphoreType.DMA
    return [dma((size_x,)), dma((size_y, size_x)), dma((size_x * size_y,))]


def scatter_scratch(size_x, size_y, rows, lanes):
    dma = pltpu.SemaphoreType.DMA
    return [
        pltpu.VMEM((size_y, size_x, rows, lanes), jnp.float32),
        pltpu.VMEM((size_x, rows, lanes), jnp.float32),
        pltpu.VMEM((size_x, rows, lanes), jnp.float32),
        dma((size_y, size_x)),
        dma((size_y, size_x)),
        dma((size_x,)),
        dma((size_x,)),
    ]


def gather_kernel(
    sizes,
    owner_ref,
    cell_ref,
    diam_ref,
    vel_ref,
    vel_all,
    void_all,
    void_own,
    base_ref,
    partial_ref,
    solid_ref,
    solid_all,
    my_edge,
    edges,
    vel_lo,
    vel_hi,
    edge_send,
    edge_recv,
    side_send,
    side_recv,
    *rest,
):
    size_x, size_y, size_z, bx, by = sizes
    owners = size_x * size_y
    row_count, lane_count = partial_ref.shape[1:]
    plane = Plane(size_x, size_y)
    gx, gy, gz, me = plane.gx, plane.gy, plane.gz, plane.me
    above, below = lax.rem(gz + 1, size_z), lax.rem(gz + size_z - 1, size_z)

    def slot(owner):
        return solid_all.at[owner // size_y + 1, lax.rem(owner, size_y) + 1]

    def place(r, other):
        owner = lax.rem(me + r, owners)
        return (owner // size_y, lax.rem(owner, size_y), other)

    barrier = pltpu.get_barrier_semaphore()
    greeted = plane.greet(barrier)
    each(0, owners, lambda r: signal(barrier, place(r, above)))
    each(0, owners, lambda r: signal(barrier, place(r, below)))
    solid_all[...] = jnp.zeros_like(solid_all)
    vel_all[me] = vel_ref[...]
    pl.semaphore_wait(barrier, greeted + 2 * owners)

    vel = Gather(plane, vel_ref, lambda owner: vel_all.at[owner], *rest[:3])
    solid_gather = Gather(plane, slot(me), slot, *rest[3:6])
    scatter = Scatter(plane, partial_ref, *rest[6:])

    def edge_copy(r, mine, side):
        there = lax.rem(me + r, owners)
        return remote(
            my_edge.at[side],
            edges.at[side, mine],
            edge_send.at[side, there],
            edge_recv.at[side, mine],
            place(r, (above, below)[side]),
        )

    sides = (
        remote(
            vel_ref.at[:, pl.ds(lane_count - 128, 128)],
            vel_lo,
            side_send.at[0],
            side_recv.at[0],
            (gx, gy, above),
        ),
        remote(
            vel_ref.at[:, pl.ds(0, 128)], vel_hi, side_send.at[1], side_recv.at[1], (gx, gy, below)
        ),
    )
    vel.start()
    for copy in sides:
        copy.start()
    deposit_volume(owner_ref, cell_ref, diam_ref, partial_ref)
    scatter.start()
    vel.forward(1, size_x - 1)
    scatter.forward()
    vel.forward(size_x - 1, size_x)
    scatter.total(solid_ref)
    solid = solid_ref[...]
    slot(me)[...] = solid.reshape(bx, by, lane_count)
    solid_gather.start()
    rows_at = lax.broadcasted_iota(jnp.int32, (row_count, 128), 0)
    lanes_at = lax.broadcasted_iota(jnp.int32, (row_count, 128), 1)
    for side, column in enumerate((solid[:, lane_count - 1 :], solid[:, :1])):
        my_edge[side] = jnp.sum(
            jnp.where(rows_at == lanes_at, column, 0.0), axis=0, keepdims=True
        )
        each(0, owners, lambda r, side=side: edge_copy(r, me, side).start())
    solid_gather.forward(1, size_x)

    vel.wait()
    for copy in sides:
        copy.wait_recv()
    own = vel_ref[...]
    own4 = own.reshape(3, bx, by, lane_count)

    def beside(owner, there):
        brick = vel_all[jnp.where(there, owner, me)].reshape(3, bx, by, lane_count)
        return jnp.where(there, brick, 0.0)

    x_before = beside(me - size_y, gx > 0)[:, bx - 1 :]
    x_after = beside(me + size_y, gx < size_x - 1)[:, :1]
    y_before = beside(me - 1, gy > 0)[:, :, by - 1 :]
    y_after = beside(me + 1, gy < size_y - 1)[:, :, :1]
    z_before = jnp.where(gz > 0, vel_lo[:, 127:], 0.0)
    z_after = jnp.where(gz < size_z - 1, vel_hi[:, :1], 0.0)
    total = shifted(own4, 1, -1, x_after) + shifted(own4, 1, 1, x_before)
    total = total + shifted(own4, 2, -1, y_after) + shifted(own4, 2, 1, y_before)
    total = total.reshape(3 * row_count, lane_count)
    total = total + lane_shifted(own, -1, z_after) + lane_shifted(own, 1, z_before)
    base_ref[...] = own + TIME_STEP * (total - 6.0 * own)

    solid_gather.wait()
    for side in range(2):
        each(0, owners, lambda r, side=side: edge_copy(0, r, side).wait_recv())

    def fill_brick(owner):
        ox, oy = owner // size_y + 1, lax.rem(owner, size_y) + 1
        cells = solid_all[ox, oy]
        flat = cells.reshape(row_count, lane_count)
        ends = []
        for side, inside in ((0, gz > 0), (1, gz < size_z - 1)):
            line = edges[side, owner]
            column = jnp.sum(jnp.where(rows_at == lanes_at, line, 0.0), axis=1, keepdims=True)
            ends.append(jnp.where(inside, column, 0.0))
        near = shifted(cells, 0, -1, solid_all[ox + 1, oy][:1])
        near = near + shifted(cells, 0, 1, solid_all[ox - 1, oy][bx - 1 :])
        near = near + shifted(cells, 1, -1, solid_all[ox, oy + 1][:, :1])
        near = near + shifted(cells, 1, 1, solid_all[ox, oy - 1][:, by - 1 :])
        near = near.reshape(row_count, lane_count)
        near = near + lane_shifted(flat, -1, ends[1]) + lane_shifted(flat, 1, ends[0])
        smooth = (flat + SPREAD * near) / (1.0 + 6 * SPREAD)
        void_all[owner] = jnp.maximum(1.0 - smooth, VOID_FLOOR)

    each(0, owners, fill_brick)
    void_own[...] = void_all[me]

    for copy in sides:
        copy.wait_send()
    for side in range(2):
        each(0, owners, lambda r, side=side: edge_copy(r, me, side).wait_send())
    vel.finish()
    scatter.finish()
    solid_gather.finish()


def source_kernel(sizes, part_ref, out_ref, *rest):
    plane = Plane(*sizes)
    barrier = pltpu.get_barrier_semaphore()
    pl.semaphore_wait(barrier, plane.greet(barrier))
    scatter = Scatter(plane, part_ref, *rest)
    scatter.start()
    scatter.forward()
    scatter.total(out_ref)
    scatter.finish()


def per_device(fluid_velocity, particle_velocity, diameter, particle_cell, block_owner):
    size_x, size_y, size_z = (lax.axis_size(name) for name in ("gx", "gy", "gz"))
    owners = size_x * size_y
    bx, by, lane_count = fluid_velocity.shape[1:]
    row_count = bx * by
    owner_list = block_owner[:, 0]
    vmem = pl.BlockSpec(memory_space=VMEM)
    smem = pl.BlockSpec(memory_space=SMEM)
    limit = 56 * 1024 * 1024

    def full(*shape):
        return jax.ShapeDtypeStruct(shape, jnp.float32)

    dma = pltpu.SemaphoreType.DMA
    vel_all, void_all, void_own, base = pl.pallas_call(
        functools.partial(gather_kernel, (size_x, size_y, size_z, bx, by)),
        out_shape=(
            full(owners, 3 * row_count, lane_count),
            full(owners, row_count, lane_count),
            full(row_count, lane_count),
            full(3 * row_count, lane_count),
        ),
        in_specs=[smem] + [vmem] * 3,
        out_specs=(vmem,) * 4,
        scratch_shapes=[
            pltpu.VMEM((owners, row_count, lane_count), jnp.float32),
            pltpu.VMEM((row_count, lane_count), jnp.float32),
            pltpu.VMEM((size_x + 2, size_y + 2, bx, by, lane_count), jnp.float32),
            pltpu.VMEM((2, 1, 128), jnp.float32),
            pltpu.VMEM((2, owners, 1, 128), jnp.float32),
            pltpu.VMEM((3 * row_count, 128), jnp.float32),
            pltpu.VMEM((3 * row_count, 128), jnp.float32),
            dma((2, owners)),
            dma((2, owners)),
            dma((2,)),
            dma((2,)),
        ]
        + gather_sems(size_x, size_y) * 2
        + scatter_scratch(size_x, size_y, row_count, lane_count),
        compiler_params=pltpu.CompilerParams(
            vmem_limit_bytes=limit, collective_id=0, has_side_effects=True
        ),
        name="gather_plane",
    )(
        owner_list,
        particle_cell,
        diameter,
        fluid_velocity.reshape(3 * row_count, lane_count),
    )

    accel, force_part, voidage = pl.pallas_call(
        force_kernel,
        out_shape=(
            full(3, *diameter.shape),
            full(owners, 3 * row_count, lane_count),
            full(row_count, lane_count),
        ),
        in_specs=[smem] + [vmem] * 6,
        out_specs=(vmem,) * 3,
        scratch_shapes=[pltpu.VMEM((owners, 8 * row_count, lane_count), jnp.bfloat16)],
        compiler_params=pltpu.CompilerParams(vmem_limit_bytes=limit),
        name="force_deposit",
    )(owner_list, particle_cell, diameter, particle_velocity.transpose(1, 0, 2), vel_all, void_all, void_own)

    total = pl.pallas_call(
        functools.partial(source_kernel, (size_x, size_y)),
        out_shape=full(3 * row_count, lane_count),
        in_specs=[vmem],
        out_specs=vmem,
        scratch_shapes=scatter_scratch(size_x, size_y, 3 * row_count, lane_count),
        compiler_params=pltpu.CompilerParams(
            vmem_limit_bytes=limit, collective_id=1, has_side_effects=True
        ),
        name="sum_source",
    )(force_part)
    voidage = voidage.reshape(bx, by, lane_count)
    brick = (3, bx, by, lane_count)
    weight = TIME_STEP / (FLUID_DENSITY * voidage)
    fluid_next = base.reshape(brick) - total.reshape(brick) * weight[None]
    return (
        accel.transpose(1, 0, 2),
        voidage,
        fluid_next,
    )


def solution(mesh):
    placed = (
        P(None, "gx", "gy", "gz"),
        P(("gx", "gy", "gz"), None, None),
        P(("gx", "gy", "gz"), None),
        P(("gx", "gy", "gz"), None),
        P(("gx", "gy", "gz"), None),
    )
    return jax.shard_map(
        per_device,
        mesh=mesh,
        in_specs=placed,
        out_specs=(
            P(("gx", "gy", "gz"), None, None),
            P("gx", "gy", "gz"),
            P(None, "gx", "gy", "gz"),
        ),
        check_vma=False,
    )
```

```python
import functools
import math

import jax
import jax.numpy as jnp
from jax import lax
from jax.experimental import pallas as pl
from jax.experimental.pallas import tpu as pltpu
from jax.sharding import PartitionSpec as P

VISCOSITY = 0.1
FLUID_DENSITY = 0.05
SOLID_DENSITY = 2.5
TIME_STEP = 0.05
VOID_FLOOR = 0.35
SPREAD = 0.1
GROUP = 8
PLANE = ("gx", "gy")
VMEM = pltpu.MemorySpace.VMEM
SMEM = pltpu.MemorySpace.SMEM


def halves(value):
    high = value.astype(jnp.bfloat16)
    low = (value - high.astype(jnp.float32)).astype(jnp.bfloat16)
    return high, low


def lane_onehot(cell_row, lane_count, per_block):
    lanes = lax.broadcasted_iota(jnp.int32, (lane_count, per_block), 0)
    hit = lanes == (cell_row & (lane_count - 1))
    return jnp.where(hit, 1.0, 0.0).astype(jnp.bfloat16)


def row_hits(cell_row, row_count, lane_count, per_block):
    rows = lax.broadcasted_iota(jnp.int32, (row_count, per_block), 0)
    return rows == lax.shift_right_logical(cell_row, lane_count.bit_length() - 1)


def spread_rows(hits, values):
    pieces = [halves(value) for value in values]
    stacked = [jnp.where(hits, part[0].astype(jnp.float32), 0.0) for part in pieces]
    stacked += [jnp.where(hits, part[1].astype(jnp.float32), 0.0) for part in pieces]
    return jnp.concatenate(stacked, axis=0).astype(jnp.bfloat16)


def onto_cells(rows, lane_hot):
    both = lax.dot_general(
        rows, lane_hot, (((1,), (1,)), ((), ())), preferred_element_type=jnp.float32
    )
    half = both.shape[0] // 2
    return both[:half] + both[half:]


def deposit_volume(owner_ref, cell_ref, diam_ref, out_ref):
    blocks, per_block = cell_ref.shape
    owners, row_count, lane_count = out_ref.shape
    dense = GROUP * row_count
    shift = lane_count.bit_length() - 1
    out_ref[...] = jnp.zeros_like(out_ref)

    def step(index):
        group, bunch = index // (owners // GROUP), lax.rem(index, owners // GROUP)
        start = pl.multiple_of(group * GROUP, GROUP)
        cells = cell_ref[pl.ds(start, GROUP), :]
        diam = diam_ref[pl.ds(start, GROUP), :]
        volume = math.pi / 6 * diam * diam * diam
        ids = lax.broadcasted_iota(jnp.int32, (dense, per_block), 0) + bunch * dense
        rows, hots = [], []
        for i in range(GROUP):
            row = cells[i : i + 1]
            at = owner_ref[start + i] * row_count + lax.shift_right_logical(row, shift)
            rows.append(spread_rows(ids == at, [volume[i : i + 1]]))
            hots.append(lane_onehot(row, lane_count, per_block))
        add = onto_cells(jnp.concatenate(rows, axis=1), jnp.concatenate(hots, axis=1))
        into = pl.ds(bunch * GROUP, GROUP)
        out_ref[into] = out_ref[into] + add.reshape(GROUP, row_count, lane_count)

    each(0, (blocks // GROUP) * (owners // GROUP), step)


def force_kernel(
    owner_ref,
    cell_ref,
    diam_ref,
    part_ref,
    vel_ref,
    void_ref,
    own_ref,
    accel_ref,
    force_ref,
    void_out,
    table,
):
    blocks, per_block = cell_ref.shape
    owners, row_count, lane_count = void_ref.shape
    void_out[...] = own_ref[...]

    @pl.loop(0, owners)
    def _(owner):
        both = jnp.concatenate([vel_ref[owner], void_ref[owner]], axis=0)
        high, low = halves(both)
        table[owner] = jnp.concatenate([high, low], axis=0)

    @pl.loop(0, blocks // GROUP)
    def _(group):
        start = pl.multiple_of(group * GROUP, GROUP)
        cells = cell_ref[pl.ds(start, GROUP), :]
        diam = diam_ref[pl.ds(start, GROUP), :]
        looked = [[], [], [], []]
        for i in range(GROUP):
            row = cells[i : i + 1]
            hot = lane_onehot(row, lane_count, per_block)
            hits = row_hits(row, row_count, lane_count, per_block)
            both = jnp.dot(
                table[owner_ref[start + i]], hot, preferred_element_type=jnp.float32
            )
            half = both.shape[0] // 2
            both = both[:half] + both[half:]
            for comp in range(4):
                piece = both[comp * row_count : (comp + 1) * row_count]
                looked[comp].append(
                    jnp.sum(jnp.where(hits, piece, 0.0), axis=0, keepdims=True)
                )
        at = [jnp.concatenate(rows, axis=0) for rows in looked]
        slip = [at[comp] - part_ref[comp, pl.ds(start, GROUP), :] for comp in range(3)]
        void_at = at[3]
        speed = jnp.sqrt(slip[0] * slip[0] + slip[1] * slip[1] + slip[2] * slip[2])
        reynolds = jnp.maximum(void_at * diam * speed / VISCOSITY, 1.0)
        drag_coeff = 0.63 + 4.8 / jnp.sqrt(reynolds)
        drag_coeff = drag_coeff * drag_coeff
        gap = 1.5 - jnp.log(reynolds) * (1.0 / math.log(10.0))
        chi_exp = 3.7 - 0.65 * jnp.exp(-0.5 * gap * gap)
        magnitude = 0.5 * drag_coeff * FLUID_DENSITY * (math.pi / 4) * diam * diam
        magnitude = magnitude * jnp.exp((2.0 - chi_exp) * jnp.log(void_at)) * speed
        force = [magnitude * slip[comp] for comp in range(3)]
        mass = SOLID_DENSITY * (math.pi / 6 * diam * diam * diam)
        for comp in range(3):
            accel_ref[comp, pl.ds(start, GROUP), :] = force[comp] / mass
            force_ref[comp, pl.ds(start, GROUP), :] = force[comp]


def each(first, last, body):
    def step(i, carry):
        body(i)
        return carry

    lax.fori_loop(first, last, step, 0)


def remote(src, dst, send_sem, recv_sem, device):
    return pltpu.make_async_remote_copy(
        src_ref=src,
        dst_ref=dst,
        send_sem=send_sem,
        recv_sem=recv_sem,
        device_id=device,
        device_id_type=pl.DeviceIdType.MESH,
    )


def signal(semaphore, device):
    pl.semaphore_signal(
        semaphore, inc=1, device_id=device, device_id_type=pl.DeviceIdType.MESH
    )


def shifted(cells, axis, step, outside):
    size = cells.shape[axis]
    if step > 0:
        kept = lax.slice_in_dim(cells, 0, size - 1, axis=axis)
        return jnp.concatenate([outside, kept], axis=axis)
    kept = lax.slice_in_dim(cells, 1, size, axis=axis)
    return jnp.concatenate([kept, outside], axis=axis)


def lane_shifted(cells, step, outside):
    size = cells.shape[1]
    lanes = lax.broadcasted_iota(jnp.int32, cells.shape, 1)
    free = 0 if step > 0 else size - 1
    return jnp.where(lanes == free, outside, pltpu.roll(cells, step % size, axis=1))


class Plane:
    def __init__(self, size_x, size_y):
        self.size_x, self.size_y = size_x, size_y
        self.gx, self.gy, self.gz = (lax.axis_index(name) for name in ("gx", "gy", "gz"))
        self.me = self.owner(self.gx, self.gy)

    def owner(self, x, y):
        return x * self.size_y + y

    def others_x(self, body):
        each(1, self.size_x, lambda r: body(lax.rem(self.gx + r, self.size_x)))

    def others_y(self, body):
        each(1, self.size_y, lambda r: body(lax.rem(self.gy + r, self.size_y)))

    def greet(self, barrier):
        self.others_x(lambda x: signal(barrier, (x, self.gy, self.gz)))
        self.others_y(lambda y: signal(barrier, (self.gx, y, self.gz)))
        return self.size_x + self.size_y - 2


class Gather:
    def __init__(self, plane, source, slot, send_x, send_y, recv):
        self.plane, self.source, self.slot = plane, source, slot
        self.send_x, self.send_y, self.recv = send_x, send_y, recv

    def along_x(self, x, owner):
        p = self.plane
        return remote(
            self.source,
            self.slot(owner),
            self.send_x.at[x],
            self.recv.at[owner],
            (x, p.gy, p.gz),
        )

    def along_y(self, x, y, owner):
        p = self.plane
        return remote(
            self.slot(owner),
            self.slot(owner),
            self.send_y.at[y, x],
            self.recv.at[owner],
            (p.gx, y, p.gz),
        )

    def start(self):
        p = self.plane
        p.others_x(lambda x: self.along_x(x, p.me).start())
        p.others_y(lambda y: self.along_y(p.gx, y, p.me).start())

    def forward(self, first, last):
        p = self.plane

        def pass_on(r):
            x = lax.rem(p.gx + p.size_x - r, p.size_x)
            owner = p.owner(x, p.gy)
            self.along_x(x, owner).wait_recv()
            p.others_y(lambda y: self.along_y(x, y, owner).start())

        each(first, last, pass_on)

    def wait(self):
        p = self.plane

        def arrive(y):
            def one(r):
                x = lax.rem(p.gx + r, p.size_x)
                self.along_y(x, y, p.owner(x, y)).wait_recv()

            each(0, p.size_x, one)

        p.others_y(arrive)

    def finish(self):
        p = self.plane
        p.others_x(lambda x: self.along_x(x, p.me).wait_send())

        def one(x):
            p.others_y(lambda y: self.along_y(x, y, p.owner(x, p.gy)).wait_send())

        each(0, p.size_x, one)


class Scatter:
    def __init__(self, plane, source, first, middle, last, send_y, recv_y, send_x, recv_x):
        self.plane, self.source = plane, source
        self.first, self.middle, self.last = first, middle, last
        self.send_y, self.recv_y, self.send_x, self.recv_x = send_y, recv_y, send_x, recv_x

    def along_y(self, x, y, mine):
        p = self.plane
        return remote(
            self.source.at[p.owner(x, y)],
            self.first.at[mine, x],
            self.send_y.at[y, x],
            self.recv_y.at[mine, x],
            (p.gx, y, p.gz),
        )

    def along_x(self, x, mine):
        p = self.plane
        return remote(
            self.middle.at[x],
            self.last.at[mine],
            self.send_x.at[x],
            self.recv_x.at[mine],
            (x, p.gy, p.gz),
        )

    def start_one(self, x):
        p = self.plane
        p.others_y(lambda y: self.along_y(x, y, p.gy).start())

    def start(self):
        self.plane.others_x(self.start_one)
        self.start_one(self.plane.gx)

    def add_one(self, x):
        p = self.plane
        self.middle[x] = self.source[p.owner(x, p.gy)]

        def add(y):
            self.along_y(x, y, y).wait_recv()
            self.middle[x] = self.middle[x] + self.first[y, x]

        p.others_y(add)

    def forward_one(self, x):
        self.add_one(x)
        self.along_x(x, self.plane.gx).start()

    def forward(self):
        self.plane.others_x(self.forward_one)
        self.add_one(self.plane.gx)

    def total(self, out_ref):
        p = self.plane
        out_ref[...] = self.middle[p.gx]

        def add(x):
            self.along_x(x, x).wait_recv()
            out_ref[...] = out_ref[...] + self.last[x]

        p.others_x(add)

    def finish(self):
        p = self.plane

        def one(x):
            p.others_y(lambda y: self.along_y(x, y, p.gy).wait_send())

        each(0, p.size_x, one)
        p.others_x(lambda x: self.along_x(x, p.gx).wait_send())


def gather_sems(size_x, size_y):
    dma = pltpu.SemaphoreType.DMA
    return [dma((size_x,)), dma((size_y, size_x)), dma((size_x * size_y,))]


def scatter_scratch(size_x, size_y, rows, lanes):
    dma = pltpu.SemaphoreType.DMA
    return [
        pltpu.VMEM((size_y, size_x, rows, lanes), jnp.float32),
        pltpu.VMEM((size_x, rows, lanes), jnp.float32),
        pltpu.VMEM((size_x, rows, lanes), jnp.float32),
        dma((size_y, size_x)),
        dma((size_y, size_x)),
        dma((size_x,)),
        dma((size_x,)),
    ]


def gather_kernel(
    sizes,
    owner_ref,
    cell_ref,
    diam_ref,
    vel_ref,
    vel_all,
    void_all,
    void_own,
    base_ref,
    partial_ref,
    solid_ref,
    solid_all,
    my_edge,
    edges,
    vel_lo,
    vel_hi,
    edge_send,
    edge_recv,
    side_send,
    side_recv,
    *rest,
):
    size_x, size_y, size_z, bx, by = sizes
    owners = size_x * size_y
    row_count, lane_count = partial_ref.shape[1:]
    plane = Plane(size_x, size_y)
    gx, gy, gz, me = plane.gx, plane.gy, plane.gz, plane.me
    above, below = lax.rem(gz + 1, size_z), lax.rem(gz + size_z - 1, size_z)

    def slot(owner):
        return solid_all.at[owner // size_y + 1, lax.rem(owner, size_y) + 1]

    def place(r, other):
        owner = lax.rem(me + r, owners)
        return (owner // size_y, lax.rem(owner, size_y), other)

    barrier = pltpu.get_barrier_semaphore()
    greeted = plane.greet(barrier)
    each(0, owners, lambda r: signal(barrier, place(r, above)))
    each(0, owners, lambda r: signal(barrier, place(r, below)))
    solid_all[...] = jnp.zeros_like(solid_all)
    vel_all[me] = vel_ref[...]
    pl.semaphore_wait(barrier, greeted + 2 * owners)

    vel = Gather(plane, vel_ref, lambda owner: vel_all.at[owner], *rest[:3])
    solid_gather = Gather(plane, slot(me), slot, *rest[3:6])
    scatter = Scatter(plane, partial_ref, *rest[6:])

    def edge_copy(r, mine, side):
        there = lax.rem(me + r, owners)
        return remote(
            my_edge.at[side],
            edges.at[side, mine],
            edge_send.at[side, there],
            edge_recv.at[side, mine],
            place(r, (above, below)[side]),
        )

    sides = (
        remote(
            vel_ref.at[:, pl.ds(lane_count - 128, 128)],
            vel_lo,
            side_send.at[0],
            side_recv.at[0],
            (gx, gy, above),
        ),
        remote(
            vel_ref.at[:, pl.ds(0, 128)], vel_hi, side_send.at[1], side_recv.at[1], (gx, gy, below)
        ),
    )
    vel.start()
    for copy in sides:
        copy.start()
    deposit_volume(owner_ref, cell_ref, diam_ref, partial_ref)
    scatter.start()
    vel.forward(1, size_x - 1)
    scatter.forward()
    vel.forward(size_x - 1, size_x)
    scatter.total(solid_ref)
    solid = solid_ref[...]
    slot(me)[...] = solid.reshape(bx, by, lane_count)
    solid_gather.start()
    rows_at = lax.broadcasted_iota(jnp.int32, (row_count, 128), 0)
    lanes_at = lax.broadcasted_iota(jnp.int32, (row_count, 128), 1)
    for side, column in enumerate((solid[:, lane_count - 1 :], solid[:, :1])):
        my_edge[side] = jnp.sum(
            jnp.where(rows_at == lanes_at, column, 0.0), axis=0, keepdims=True
        )
        each(0, owners, lambda r, side=side: edge_copy(r, me, side).start())
    solid_gather.forward(1, size_x)

    vel.wait()
    for copy in sides:
        copy.wait_recv()
    own = vel_ref[...]
    own4 = own.reshape(3, bx, by, lane_count)

    def beside(owner, there):
        brick = vel_all[jnp.where(there, owner, me)].reshape(3, bx, by, lane_count)
        return jnp.where(there, brick, 0.0)

    x_before = beside(me - size_y, gx > 0)[:, bx - 1 :]
    x_after = beside(me + size_y, gx < size_x - 1)[:, :1]
    y_before = beside(me - 1, gy > 0)[:, :, by - 1 :]
    y_after = beside(me + 1, gy < size_y - 1)[:, :, :1]
    z_before = jnp.where(gz > 0, vel_lo[:, 127:], 0.0)
    z_after = jnp.where(gz < size_z - 1, vel_hi[:, :1], 0.0)
    total = shifted(own4, 1, -1, x_after) + shifted(own4, 1, 1, x_before)
    total = total + shifted(own4, 2, -1, y_after) + shifted(own4, 2, 1, y_before)
    total = total.reshape(3 * row_count, lane_count)
    total = total + lane_shifted(own, -1, z_after) + lane_shifted(own, 1, z_before)
    base_ref[...] = own + TIME_STEP * (total - 6.0 * own)

    solid_gather.wait()
    for side in range(2):
        each(0, owners, lambda r, side=side: edge_copy(0, r, side).wait_recv())

    def fill_brick(owner):
        ox, oy = owner // size_y + 1, lax.rem(owner, size_y) + 1
        cells = solid_all[ox, oy]
        flat = cells.reshape(row_count, lane_count)
        ends = []
        for side, inside in ((0, gz > 0), (1, gz < size_z - 1)):
            line = edges[side, owner]
            column = jnp.sum(jnp.where(rows_at == lanes_at, line, 0.0), axis=1, keepdims=True)
            ends.append(jnp.where(inside, column, 0.0))
        near = shifted(cells, 0, -1, solid_all[ox + 1, oy][:1])
        near = near + shifted(cells, 0, 1, solid_all[ox - 1, oy][bx - 1 :])
        near = near + shifted(cells, 1, -1, solid_all[ox, oy + 1][:, :1])
        near = near + shifted(cells, 1, 1, solid_all[ox, oy - 1][:, by - 1 :])
        near = near.reshape(row_count, lane_count)
        near = near + lane_shifted(flat, -1, ends[1]) + lane_shifted(flat, 1, ends[0])
        smooth = (flat + SPREAD * near) / (1.0 + 6 * SPREAD)
        void_all[owner] = jnp.maximum(1.0 - smooth, VOID_FLOOR)

    each(0, owners, fill_brick)
    void_own[...] = void_all[me]

    for copy in sides:
        copy.wait_send()
    for side in range(2):
        each(0, owners, lambda r, side=side: edge_copy(r, me, side).wait_send())
    vel.finish()
    scatter.finish()
    solid_gather.finish()


def source_kernel(sizes, owner_ref, cell_ref, force_ref, out_ref, part_ref, hot_ref, *rest):
    size_x, size_y = sizes
    blocks, per_block = cell_ref.shape
    lane_count = out_ref.shape[1]
    row_count = out_ref.shape[0] // 3
    dense = size_y * row_count
    shift = lane_count.bit_length() - 1
    plane = Plane(size_x, size_y)
    barrier = pltpu.get_barrier_semaphore()
    greeted = plane.greet(barrier)

    def fill_hot(group):
        cells = cell_ref[pl.ds(pl.multiple_of(group * GROUP, GROUP), GROUP), :]
        hots = [lane_onehot(cells[i : i + 1], lane_count, per_block) for i in range(GROUP)]
        hot_ref[group] = jnp.concatenate(hots, axis=1)

    each(0, blocks // GROUP, fill_hot)
    part_ref[...] = jnp.zeros_like(part_ref)
    pl.semaphore_wait(barrier, greeted)
    scatter = Scatter(plane, part_ref, *rest)

    def deposit(x):
        def step(group):
            start = pl.multiple_of(group * GROUP, GROUP)
            cells = cell_ref[pl.ds(start, GROUP), :]
            force = [force_ref[comp, pl.ds(start, GROUP), :] for comp in range(3)]
            ids = lax.broadcasted_iota(jnp.int32, (dense, per_block), 0) + x * dense
            rows = []
            for i in range(GROUP):
                row = lax.shift_right_logical(cells[i : i + 1], shift)
                hits = ids == owner_ref[start + i] * row_count + row
                rows.append(spread_rows(hits, [force[comp][i : i + 1] for comp in range(3)]))
            add = onto_cells(jnp.concatenate(rows, axis=1), hot_ref[group])
            for y in range(size_y):
                owner = x * size_y + y
                for comp in range(3):
                    into = pl.ds(comp * row_count, row_count)
                    piece = add[comp * dense + y * row_count :][:row_count]
                    part_ref[owner, into, :] = part_ref[owner, into, :] + piece

        each(0, blocks // GROUP, step)

    def one_x(r):
        x = lax.rem(plane.gx + r, size_x)
        deposit(x)
        scatter.start_one(x)

        @pl.when(r > 1)
        def _():
            scatter.forward_one(lax.rem(plane.gx + r - 1, size_x))

    each(1, size_x + 1, one_x)
    scatter.add_one(plane.gx)
    scatter.total(out_ref)
    scatter.finish()


def per_device(fluid_velocity, particle_velocity, diameter, particle_cell, block_owner):
    size_x, size_y, size_z = (lax.axis_size(name) for name in ("gx", "gy", "gz"))
    owners = size_x * size_y
    bx, by, lane_count = fluid_velocity.shape[1:]
    row_count = bx * by
    owner_list = block_owner[:, 0]
    vmem = pl.BlockSpec(memory_space=VMEM)
    smem = pl.BlockSpec(memory_space=SMEM)
    limit = 56 * 1024 * 1024

    def full(*shape):
        return jax.ShapeDtypeStruct(shape, jnp.float32)

    dma = pltpu.SemaphoreType.DMA
    vel_all, void_all, void_own, base = pl.pallas_call(
        functools.partial(gather_kernel, (size_x, size_y, size_z, bx, by)),
        out_shape=(
            full(owners, 3 * row_count, lane_count),
            full(owners, row_count, lane_count),
            full(row_count, lane_count),
            full(3 * row_count, lane_count),
        ),
        in_specs=[smem] + [vmem] * 3,
        out_specs=(vmem,) * 4,
        scratch_shapes=[
            pltpu.VMEM((owners, row_count, lane_count), jnp.float32),
            pltpu.VMEM((row_count, lane_count), jnp.float32),
            pltpu.VMEM((size_x + 2, size_y + 2, bx, by, lane_count), jnp.float32),
            pltpu.VMEM((2, 1, 128), jnp.float32),
            pltpu.VMEM((2, owners, 1, 128), jnp.float32),
            pltpu.VMEM((3 * row_count, 128), jnp.float32),
            pltpu.VMEM((3 * row_count, 128), jnp.float32),
            dma((2, owners)),
            dma((2, owners)),
            dma((2,)),
            dma((2,)),
        ]
        + gather_sems(size_x, size_y) * 2
        + scatter_scratch(size_x, size_y, row_count, lane_count),
        compiler_params=pltpu.CompilerParams(
            vmem_limit_bytes=limit, collective_id=0, has_side_effects=True
        ),
        name="gather_plane",
    )(
        owner_list,
        particle_cell,
        diameter,
        fluid_velocity.reshape(3 * row_count, lane_count),
    )

    accel, force, voidage = pl.pallas_call(
        force_kernel,
        out_shape=(
            full(3, *diameter.shape),
            full(3, *diameter.shape),
            full(row_count, lane_count),
        ),
        in_specs=[smem] + [vmem] * 6,
        out_specs=(vmem,) * 3,
        scratch_shapes=[pltpu.VMEM((owners, 8 * row_count, lane_count), jnp.bfloat16)],
        compiler_params=pltpu.CompilerParams(vmem_limit_bytes=limit),
        name="force_deposit",
    )(owner_list, particle_cell, diameter, particle_velocity.transpose(1, 0, 2), vel_all, void_all, void_own)

    total = pl.pallas_call(
        functools.partial(source_kernel, (size_x, size_y)),
        out_shape=full(3 * row_count, lane_count),
        in_specs=[smem] + [vmem] * 2,
        out_specs=vmem,
        scratch_shapes=[
            pltpu.VMEM((owners, 3 * row_count, lane_count), jnp.float32),
            pltpu.VMEM(
                (diameter.shape[0] // GROUP, lane_count, GROUP * diameter.shape[1]), jnp.bfloat16
            ),
        ]
        + scatter_scratch(size_x, size_y, 3 * row_count, lane_count),
        compiler_params=pltpu.CompilerParams(
            vmem_limit_bytes=limit, collective_id=1, has_side_effects=True
        ),
        name="sum_source",
    )(owner_list, particle_cell, force)
    voidage = voidage.reshape(bx, by, lane_count)
    brick = (3, bx, by, lane_count)
    weight = TIME_STEP / (FLUID_DENSITY * voidage)
    fluid_next = base.reshape(brick) - total.reshape(brick) * weight[None]
    return (
        accel.transpose(1, 0, 2),
        voidage,
        fluid_next,
    )


def solution(mesh):
    placed = (
        P(None, "gx", "gy", "gz"),
        P(("gx", "gy", "gz"), None, None),
        P(("gx", "gy", "gz"), None),
        P(("gx", "gy", "gz"), None),
        P(("gx", "gy", "gz"), None),
    )
    return jax.shard_map(
        per_device,
        mesh=mesh,
        in_specs=placed,
        out_specs=(
            P(("gx", "gy", "gz"), None, None),
            P("gx", "gy", "gz"),
            P(None, "gx", "gy", "gz"),
        ),
        check_vma=False,
    )
```

```python
import functools
import math

import jax
import jax.numpy as jnp
from jax import lax
from jax.experimental import pallas as pl
from jax.experimental.pallas import tpu as pltpu
from jax.sharding import PartitionSpec as P

VISCOSITY = 0.1
FLUID_DENSITY = 0.05
SOLID_DENSITY = 2.5
TIME_STEP = 0.05
VOID_FLOOR = 0.35
SPREAD = 0.1
GROUP = 8
PLANE = ("gx", "gy")
VMEM = pltpu.MemorySpace.VMEM
SMEM = pltpu.MemorySpace.SMEM


def halves(value):
    high = value.astype(jnp.bfloat16)
    low = (value - high.astype(jnp.float32)).astype(jnp.bfloat16)
    return high, low


def lane_onehot(cell_row, lane_count, per_block):
    lanes = lax.broadcasted_iota(jnp.int32, (lane_count, per_block), 0)
    hit = lanes == (cell_row & (lane_count - 1))
    return jnp.where(hit, 1.0, 0.0).astype(jnp.bfloat16)


def row_hits(cell_row, row_count, lane_count, per_block):
    rows = lax.broadcasted_iota(jnp.int32, (row_count, per_block), 0)
    return rows == lax.shift_right_logical(cell_row, lane_count.bit_length() - 1)


def spread_rows(hits, values):
    pieces = [halves(value) for value in values]
    stacked = [jnp.where(hits, part[0].astype(jnp.float32), 0.0) for part in pieces]
    stacked += [jnp.where(hits, part[1].astype(jnp.float32), 0.0) for part in pieces]
    return jnp.concatenate(stacked, axis=0).astype(jnp.bfloat16)


def onto_cells(rows, lane_hot):
    both = lax.dot_general(
        rows, lane_hot, (((1,), (1,)), ((), ())), preferred_element_type=jnp.float32
    )
    half = both.shape[0] // 2
    return both[:half] + both[half:]


def deposit_volume(owner_ref, cell_ref, diam_ref, out_ref):
    blocks, per_block = cell_ref.shape
    owners, row_count, lane_count = out_ref.shape
    dense = GROUP * row_count
    shift = lane_count.bit_length() - 1
    out_ref[...] = jnp.zeros_like(out_ref)

    def step(index):
        group, bunch = index // (owners // GROUP), lax.rem(index, owners // GROUP)
        start = pl.multiple_of(group * GROUP, GROUP)
        cells = cell_ref[pl.ds(start, GROUP), :]
        diam = diam_ref[pl.ds(start, GROUP), :]
        volume = math.pi / 6 * diam * diam * diam
        ids = lax.broadcasted_iota(jnp.int32, (dense, per_block), 0) + bunch * dense
        rows, hots = [], []
        for i in range(GROUP):
            row = cells[i : i + 1]
            at = owner_ref[start + i] * row_count + lax.shift_right_logical(row, shift)
            rows.append(spread_rows(ids == at, [volume[i : i + 1]]))
            hots.append(lane_onehot(row, lane_count, per_block))
        add = onto_cells(jnp.concatenate(rows, axis=1), jnp.concatenate(hots, axis=1))
        into = pl.ds(bunch * GROUP, GROUP)
        out_ref[into] = out_ref[into] + add.reshape(GROUP, row_count, lane_count)

    each(0, (blocks // GROUP) * (owners // GROUP), step)


def force_kernel(
    owner_ref,
    cell_ref,
    diam_ref,
    part_ref,
    vel_ref,
    void_ref,
    own_ref,
    accel_ref,
    out_ref,
    void_out,
    table,
):
    blocks, per_block = cell_ref.shape
    owners, row_count, lane_count = void_ref.shape
    out_ref[...] = jnp.zeros_like(out_ref)
    void_out[...] = own_ref[...]

    @pl.loop(0, owners)
    def _(owner):
        both = jnp.concatenate([vel_ref[owner], void_ref[owner]], axis=0)
        high, low = halves(both)
        table[owner] = jnp.concatenate([high, low], axis=0)

    @pl.loop(0, blocks // GROUP)
    def _(group):
        start = pl.multiple_of(group * GROUP, GROUP)
        cells = cell_ref[pl.ds(start, GROUP), :]
        diam = diam_ref[pl.ds(start, GROUP), :]
        hots, hit_list, looked = [], [], [[], [], [], []]
        for i in range(GROUP):
            row = cells[i : i + 1]
            hot = lane_onehot(row, lane_count, per_block)
            hits = row_hits(row, row_count, lane_count, per_block)
            hots.append(hot)
            hit_list.append(hits)
            both = jnp.dot(
                table[owner_ref[start + i]], hot, preferred_element_type=jnp.float32
            )
            half = both.shape[0] // 2
            both = both[:half] + both[half:]
            for comp in range(4):
                piece = both[comp * row_count : (comp + 1) * row_count]
                looked[comp].append(
                    jnp.sum(jnp.where(hits, piece, 0.0), axis=0, keepdims=True)
                )
        at = [jnp.concatenate(rows, axis=0) for rows in looked]
        slip = [at[comp] - part_ref[comp, pl.ds(start, GROUP), :] for comp in range(3)]
        void_at = at[3]
        speed = jnp.sqrt(slip[0] * slip[0] + slip[1] * slip[1] + slip[2] * slip[2])
        reynolds = jnp.maximum(void_at * diam * speed / VISCOSITY, 1.0)
        drag_coeff = 0.63 + 4.8 / jnp.sqrt(reynolds)
        drag_coeff = drag_coeff * drag_coeff
        gap = 1.5 - jnp.log(reynolds) * (1.0 / math.log(10.0))
        chi_exp = 3.7 - 0.65 * jnp.exp(-0.5 * gap * gap)
        magnitude = 0.5 * drag_coeff * FLUID_DENSITY * (math.pi / 4) * diam * diam
        magnitude = magnitude * jnp.exp((2.0 - chi_exp) * jnp.log(void_at)) * speed
        force = [magnitude * slip[comp] for comp in range(3)]
        mass = SOLID_DENSITY * (math.pi / 6 * diam * diam * diam)
        for comp in range(3):
            accel_ref[comp, pl.ds(start, GROUP), :] = force[comp] / mass
        adds = []
        for i in range(GROUP):
            rows = spread_rows(hit_list[i], [force[comp][i : i + 1] for comp in range(3)])
            adds.append(onto_cells(rows, hots[i]))
        for i in range(GROUP):
            owner = owner_ref[start + i]
            out_ref[owner] = out_ref[owner] + adds[i]


def each(first, last, body):
    def step(i, carry):
        body(i)
        return carry

    lax.fori_loop(first, last, step, 0)


def remote(src, dst, send_sem, recv_sem, device):
    return pltpu.make_async_remote_copy(
        src_ref=src,
        dst_ref=dst,
        send_sem=send_sem,
        recv_sem=recv_sem,
        device_id=device,
        device_id_type=pl.DeviceIdType.MESH,
    )


def signal(semaphore, device):
    pl.semaphore_signal(
        semaphore, inc=1, device_id=device, device_id_type=pl.DeviceIdType.MESH
    )


def shifted(cells, axis, step, outside):
    size = cells.shape[axis]
    if step > 0:
        kept = lax.slice_in_dim(cells, 0, size - 1, axis=axis)
        return jnp.concatenate([outside, kept], axis=axis)
    kept = lax.slice_in_dim(cells, 1, size, axis=axis)
    return jnp.concatenate([kept, outside], axis=axis)


def lane_shifted(cells, step, outside):
    size = cells.shape[1]
    lanes = lax.broadcasted_iota(jnp.int32, cells.shape, 1)
    free = 0 if step > 0 else size - 1
    return jnp.where(lanes == free, outside, pltpu.roll(cells, step % size, axis=1))


class Plane:
    def __init__(self, size_x, size_y):
        self.size_x, self.size_y = size_x, size_y
        self.gx, self.gy, self.gz = (lax.axis_index(name) for name in ("gx", "gy", "gz"))
        self.me = self.owner(self.gx, self.gy)

    def owner(self, x, y):
        return x * self.size_y + y

    def others_x(self, body):
        each(1, self.size_x, lambda r: body(lax.rem(self.gx + r, self.size_x)))

    def others_y(self, body):
        each(1, self.size_y, lambda r: body(lax.rem(self.gy + r, self.size_y)))

    def greet(self, barrier):
        self.others_x(lambda x: signal(barrier, (x, self.gy, self.gz)))
        self.others_y(lambda y: signal(barrier, (self.gx, y, self.gz)))
        return self.size_x + self.size_y - 2


class Gather:
    def __init__(self, plane, source, slot, send_x, send_y, recv):
        self.plane, self.source, self.slot = plane, source, slot
        self.send_x, self.send_y, self.recv = send_x, send_y, recv

    def along_x(self, x, owner):
        p = self.plane
        return remote(
            self.source,
            self.slot(owner),
            self.send_x.at[x],
            self.recv.at[owner],
            (x, p.gy, p.gz),
        )

    def along_y(self, x, y, owner):
        p = self.plane
        return remote(
            self.slot(owner),
            self.slot(owner),
            self.send_y.at[y, x],
            self.recv.at[owner],
            (p.gx, y, p.gz),
        )

    def start(self):
        p = self.plane
        p.others_x(lambda x: self.along_x(x, p.me).start())
        p.others_y(lambda y: self.along_y(p.gx, y, p.me).start())

    def forward(self, first, last):
        p = self.plane

        def pass_on(r):
            x = lax.rem(p.gx + p.size_x - r, p.size_x)
            owner = p.owner(x, p.gy)
            self.along_x(x, owner).wait_recv()
            p.others_y(lambda y: self.along_y(x, y, owner).start())

        each(first, last, pass_on)

    def wait(self):
        p = self.plane

        def arrive(y):
            def one(r):
                x = lax.rem(p.gx + r, p.size_x)
                self.along_y(x, y, p.owner(x, y)).wait_recv()

            each(0, p.size_x, one)

        p.others_y(arrive)

    def finish(self):
        p = self.plane
        p.others_x(lambda x: self.along_x(x, p.me).wait_send())

        def one(x):
            p.others_y(lambda y: self.along_y(x, y, p.owner(x, p.gy)).wait_send())

        each(0, p.size_x, one)


class Scatter:
    def __init__(self, plane, source, first, middle, last, send_y, recv_y, send_x, recv_x):
        self.plane, self.source = plane, source
        self.first, self.middle, self.last = first, middle, last
        self.send_y, self.recv_y, self.send_x, self.recv_x = send_y, recv_y, send_x, recv_x

    def along_y(self, x, y, mine):
        p = self.plane
        return remote(
            self.source.at[p.owner(x, y)],
            self.first.at[mine, x],
            self.send_y.at[y, x],
            self.recv_y.at[mine, x],
            (p.gx, y, p.gz),
        )

    def along_x(self, x, mine):
        p = self.plane
        return remote(
            self.middle.at[x],
            self.last.at[mine],
            self.send_x.at[x],
            self.recv_x.at[mine],
            (x, p.gy, p.gz),
        )

    def start(self):
        p = self.plane

        def one(x):
            p.others_y(lambda y: self.along_y(x, y, p.gy).start())

        p.others_x(one)
        one(p.gx)

    def forward(self):
        p = self.plane

        def one(x):
            self.middle[x] = self.source[p.owner(x, p.gy)]

            def add(y):
                self.along_y(x, y, y).wait_recv()
                self.middle[x] = self.middle[x] + self.first[y, x]

            p.others_y(add)

        def send(x):
            one(x)
            self.along_x(x, p.gx).start()

        p.others_x(send)
        one(p.gx)

    def total(self, out_ref):
        p = self.plane
        out_ref[...] = self.middle[p.gx]

        def add(x):
            self.along_x(x, x).wait_recv()
            out_ref[...] = out_ref[...] + self.last[x]

        p.others_x(add)

    def finish(self):
        p = self.plane

        def one(x):
            p.others_y(lambda y: self.along_y(x, y, p.gy).wait_send())

        each(0, p.size_x, one)
        p.others_x(lambda x: self.along_x(x, p.gx).wait_send())


def gather_sems(size_x, size_y):
    dma = pltpu.SemaphoreType.DMA
    return [dma((size_x,)), dma((size_y, size_x)), dma((size_x * size_y,))]


def scatter_scratch(size_x, size_y, rows, lanes):
    dma = pltpu.SemaphoreType.DMA
    return [
        pltpu.VMEM((size_y, size_x, rows, lanes), jnp.float32),
        pltpu.VMEM((size_x, rows, lanes), jnp.float32),
        pltpu.VMEM((size_x, rows, lanes), jnp.float32),
        dma((size_y, size_x)),
        dma((size_y, size_x)),
        dma((size_x,)),
        dma((size_x,)),
    ]


def gather_kernel(
    sizes,
    owner_ref,
    cell_ref,
    diam_ref,
    vel_ref,
    vel_all,
    void_all,
    void_own,
    base_ref,
    partial_ref,
    solid_ref,
    solid_all,
    my_edge,
    edges,
    vel_lo,
    vel_hi,
    edge_send,
    edge_recv,
    side_send,
    side_recv,
    *rest,
):
    size_x, size_y, size_z, bx, by = sizes
    owners = size_x * size_y
    row_count, lane_count = partial_ref.shape[1:]
    plane = Plane(size_x, size_y)
    gx, gy, gz, me = plane.gx, plane.gy, plane.gz, plane.me
    above, below = lax.rem(gz + 1, size_z), lax.rem(gz + size_z - 1, size_z)

    def slot(owner):
        return solid_all.at[owner // size_y + 1, lax.rem(owner, size_y) + 1]

    def place(r, other):
        owner = lax.rem(me + r, owners)
        return (owner // size_y, lax.rem(owner, size_y), other)

    barrier = pltpu.get_barrier_semaphore()
    greeted = plane.greet(barrier)
    each(0, owners, lambda r: signal(barrier, place(r, above)))
    each(0, owners, lambda r: signal(barrier, place(r, below)))
    solid_all[...] = jnp.zeros_like(solid_all)
    vel_all[me] = vel_ref[...]
    pl.semaphore_wait(barrier, greeted + 2 * owners)

    vel = Gather(plane, vel_ref, lambda owner: vel_all.at[owner], *rest[:3])
    solid_gather = Gather(plane, slot(me), slot, *rest[3:6])
    scatter = Scatter(plane, partial_ref, *rest[6:])

    def edge_copy(r, mine, side):
        there = lax.rem(me + r, owners)
        return remote(
            my_edge.at[side],
            edges.at[side, mine],
            edge_send.at[side, there],
            edge_recv.at[side, mine],
            place(r, (above, below)[side]),
        )

    sides = (
        remote(
            vel_ref.at[:, pl.ds(lane_count - 128, 128)],
            vel_lo,
            side_send.at[0],
            side_recv.at[0],
            (gx, gy, above),
        ),
        remote(
            vel_ref.at[:, pl.ds(0, 128)], vel_hi, side_send.at[1], side_recv.at[1], (gx, gy, below)
        ),
    )
    vel.start()
    for copy in sides:
        copy.start()
    deposit_volume(owner_ref, cell_ref, diam_ref, partial_ref)
    scatter.start()
    vel.forward(1, size_x)
    scatter.forward()
    scatter.total(solid_ref)
    solid = solid_ref[...]
    slot(me)[...] = solid.reshape(bx, by, lane_count)
    solid_gather.start()
    rows_at = lax.broadcasted_iota(jnp.int32, (row_count, 128), 0)
    lanes_at = lax.broadcasted_iota(jnp.int32, (row_count, 128), 1)
    for side, column in enumerate((solid[:, lane_count - 1 :], solid[:, :1])):
        my_edge[side] = jnp.sum(
            jnp.where(rows_at == lanes_at, column, 0.0), axis=0, keepdims=True
        )
        each(0, owners, lambda r, side=side: edge_copy(r, me, side).start())
    solid_gather.forward(1, size_x)

    vel.wait()
    for copy in sides:
        copy.wait_recv()
    own = vel_ref[...]
    own4 = own.reshape(3, bx, by, lane_count)

    def beside(owner, there):
        brick = vel_all[jnp.where(there, owner, me)].reshape(3, bx, by, lane_count)
        return jnp.where(there, brick, 0.0)

    x_before = beside(me - size_y, gx > 0)[:, bx - 1 :]
    x_after = beside(me + size_y, gx < size_x - 1)[:, :1]
    y_before = beside(me - 1, gy > 0)[:, :, by - 1 :]
    y_after = beside(me + 1, gy < size_y - 1)[:, :, :1]
    z_before = jnp.where(gz > 0, vel_lo[:, 127:], 0.0)
    z_after = jnp.where(gz < size_z - 1, vel_hi[:, :1], 0.0)
    total = shifted(own4, 1, -1, x_after) + shifted(own4, 1, 1, x_before)
    total = total + shifted(own4, 2, -1, y_after) + shifted(own4, 2, 1, y_before)
    total = total.reshape(3 * row_count, lane_count)
    total = total + lane_shifted(own, -1, z_after) + lane_shifted(own, 1, z_before)
    base_ref[...] = own + TIME_STEP * (total - 6.0 * own)

    solid_gather.wait()
    for side in range(2):
        each(0, owners, lambda r, side=side: edge_copy(0, r, side).wait_recv())

    def fill_brick(owner):
        ox, oy = owner // size_y + 1, lax.rem(owner, size_y) + 1
        cells = solid_all[ox, oy]
        flat = cells.reshape(row_count, lane_count)
        ends = []
        for side, inside in ((0, gz > 0), (1, gz < size_z - 1)):
            line = edges[side, owner]
            column = jnp.sum(jnp.where(rows_at == lanes_at, line, 0.0), axis=1, keepdims=True)
            ends.append(jnp.where(inside, column, 0.0))
        near = shifted(cells, 0, -1, solid_all[ox + 1, oy][:1])
        near = near + shifted(cells, 0, 1, solid_all[ox - 1, oy][bx - 1 :])
        near = near + shifted(cells, 1, -1, solid_all[ox, oy + 1][:, :1])
        near = near + shifted(cells, 1, 1, solid_all[ox, oy - 1][:, by - 1 :])
        near = near.reshape(row_count, lane_count)
        near = near + lane_shifted(flat, -1, ends[1]) + lane_shifted(flat, 1, ends[0])
        smooth = (flat + SPREAD * near) / (1.0 + 6 * SPREAD)
        void_all[owner] = jnp.maximum(1.0 - smooth, VOID_FLOOR)

    each(0, owners, fill_brick)
    void_own[...] = void_all[me]

    for copy in sides:
        copy.wait_send()
    for side in range(2):
        each(0, owners, lambda r, side=side: edge_copy(r, me, side).wait_send())
    vel.finish()
    scatter.finish()
    solid_gather.finish()


def source_kernel(sizes, part_ref, out_ref, *rest):
    plane = Plane(*sizes)
    barrier = pltpu.get_barrier_semaphore()
    pl.semaphore_wait(barrier, plane.greet(barrier))
    scatter = Scatter(plane, part_ref, *rest)
    scatter.start()
    scatter.forward()
    scatter.total(out_ref)
    scatter.finish()


def last_kernel(base_ref, total_ref, void_ref, out_ref):
    weight = TIME_STEP / (FLUID_DENSITY * void_ref[...])
    out_ref[...] = base_ref[...] - total_ref[...] * weight[None]


def per_device(fluid_velocity, particle_velocity, diameter, particle_cell, block_owner):
    size_x, size_y, size_z = (lax.axis_size(name) for name in ("gx", "gy", "gz"))
    owners = size_x * size_y
    bx, by, lane_count = fluid_velocity.shape[1:]
    row_count = bx * by
    owner_list = block_owner[:, 0]
    vmem = pl.BlockSpec(memory_space=VMEM)
    smem = pl.BlockSpec(memory_space=SMEM)
    limit = 56 * 1024 * 1024

    def full(*shape):
        return jax.ShapeDtypeStruct(shape, jnp.float32)

    dma = pltpu.SemaphoreType.DMA
    vel_all, void_all, void_own, base = pl.pallas_call(
        functools.partial(gather_kernel, (size_x, size_y, size_z, bx, by)),
        out_shape=(
            full(owners, 3 * row_count, lane_count),
            full(owners, row_count, lane_count),
            full(row_count, lane_count),
            full(3 * row_count, lane_count),
        ),
        in_specs=[smem] + [vmem] * 3,
        out_specs=(vmem,) * 4,
        scratch_shapes=[
            pltpu.VMEM((owners, row_count, lane_count), jnp.float32),
            pltpu.VMEM((row_count, lane_count), jnp.float32),
            pltpu.VMEM((size_x + 2, size_y + 2, bx, by, lane_count), jnp.float32),
            pltpu.VMEM((2, 1, 128), jnp.float32),
            pltpu.VMEM((2, owners, 1, 128), jnp.float32),
            pltpu.VMEM((3 * row_count, 128), jnp.float32),
            pltpu.VMEM((3 * row_count, 128), jnp.float32),
            dma((2, owners)),
            dma((2, owners)),
            dma((2,)),
            dma((2,)),
        ]
        + gather_sems(size_x, size_y) * 2
        + scatter_scratch(size_x, size_y, row_count, lane_count),
        compiler_params=pltpu.CompilerParams(
            vmem_limit_bytes=limit, collective_id=0, has_side_effects=True
        ),
        name="gather_plane",
    )(
        owner_list,
        particle_cell,
        diameter,
        fluid_velocity.reshape(3 * row_count, lane_count),
    )

    accel, force_part, voidage = pl.pallas_call(
        force_kernel,
        out_shape=(
            full(3, *diameter.shape),
            full(owners, 3 * row_count, lane_count),
            full(row_count, lane_count),
        ),
        in_specs=[smem] + [vmem] * 6,
        out_specs=(vmem,) * 3,
        scratch_shapes=[pltpu.VMEM((owners, 8 * row_count, lane_count), jnp.bfloat16)],
        compiler_params=pltpu.CompilerParams(vmem_limit_bytes=limit),
        name="force_deposit",
    )(owner_list, particle_cell, diameter, particle_velocity.transpose(1, 0, 2), vel_all, void_all, void_own)

    total = pl.pallas_call(
        functools.partial(source_kernel, (size_x, size_y)),
        out_shape=full(3 * row_count, lane_count),
        in_specs=[vmem],
        out_specs=vmem,
        scratch_shapes=scatter_scratch(size_x, size_y, 3 * row_count, lane_count),
        compiler_params=pltpu.CompilerParams(
            vmem_limit_bytes=limit, collective_id=1, has_side_effects=True
        ),
        name="sum_source",
    )(force_part)
    voidage = voidage.reshape(bx, by, lane_count)
    brick = (3, bx, by, lane_count)
    fluid_next = pl.pallas_call(
        last_kernel,
        out_shape=full(3, row_count, lane_count),
        in_specs=[vmem] * 3,
        out_specs=vmem,
        compiler_params=pltpu.CompilerParams(vmem_limit_bytes=limit),
        name="last_step",
    )(base.reshape(3, row_count, lane_count), total.reshape(3, row_count, lane_count), void_own)
    fluid_next = fluid_next.reshape(brick)
    return (
        accel.transpose(1, 0, 2),
        voidage,
        fluid_next,
    )


def solution(mesh):
    placed = (
        P(None, "gx", "gy", "gz"),
        P(("gx", "gy", "gz"), None, None),
        P(("gx", "gy", "gz"), None),
        P(("gx", "gy", "gz"), None),
        P(("gx", "gy", "gz"), None),
    )
    return jax.shard_map(
        per_device,
        mesh=mesh,
        in_specs=placed,
        out_specs=(
            P(("gx", "gy", "gz"), None, None),
            P("gx", "gy", "gz"),
            P(None, "gx", "gy", "gz"),
        ),
        check_vma=False,
    )
```
